32 devices in a mesh: fsdp: 4 (over y, x), ctx: 2 (over core), tp: 4 (over z).
Axes of the slice: x: 2, y: 2, z: 4, core: 2. Of those that a mesh axis runs over, the one named last changes fastest.
Arguments:
- tokens: bfloat16 [16384, 1024], P(('fsdp', 'ctx')), may hold values from -6 to 6
- norm_gain: bfloat16 [1024], P(('fsdp', 'ctx')), may hold values from 0.5 to 1.5
- inner_weight: bfloat16 [2, 1024, 2048], P(None, ('fsdp', 'ctx'), 'tp'), may hold values from -0.1875 to 0.1875
- state_weight: bfloat16 [1024, 256], P(('fsdp', 'ctx')), may hold values from -0.1875 to 0.1875
- step_weight: bfloat16 [1024, 32], P(('fsdp', 'ctx'), 'tp'), may hold values from -0.1875 to 0.1875
- inner_taps: float32 [5, 2048], P(None, 'tp'), may hold values from -3 to 3
- state_taps: float32 [5, 256], replicated, may hold values from -3 to 3
- step_bias: float32 [32], P('tp'), may hold values from -4 to -1
- log_rate: float32 [32], P('tp'), may hold values from -2.5 to 1.5
- skip_gain: float32 [32], P('tp'), may hold values from 0.5 to 1.5
- gated_gain: float32 [2048], P('tp'), may hold values from 0.5 to 1.5
- out_weight: bfloat16 [2048, 1024], P('tp', ('fsdp', 'ctx')), may hold values from -0.125 to 0.125
- out_grad: bfloat16 [16384, 1024], P(('fsdp', 'ctx')), may hold values from -6 to 6
- positions: int32 [16384], P(('fsdp', 'ctx')), may hold values from -1 to 4095, as said below
Outputs:
- mixed_out: bfloat16 [16384, 1024], P(('fsdp', 'ctx'))
- tokens_grad: float32 [16384, 1024], P(('fsdp', 'ctx'))
- norm_gain_grad: float32 [1024], P(('fsdp', 'ctx'))
- inner_weight_grad: float32 [2, 1024, 2048], P(None, ('fsdp', 'ctx'), 'tp')
- state_weight_grad: float32 [1024, 256], P(('fsdp', 'ctx'))
- step_weight_grad: float32 [1024, 32], P(('fsdp', 'ctx'), 'tp')
- inner_taps_grad: float32 [5, 2048], P(None, 'tp')
- state_taps_grad: float32 [5, 256], replicated
- step_bias_grad: float32 [32], P('tp')
- log_rate_grad: float32 [32], P('tp')
- skip_gain_grad: float32 [32], P('tp')
- gated_gain_grad: float32 [2048], P('tp')
- out_weight_grad: float32 [2048, 1024], P('tp', ('fsdp', 'ctx'))
The draws below stay inside these ranges and needn't reach their ends.
Inputs may be any that keep to these rules, and one draw needn't show every extreme that they name: `positions`: within each fsdp index's 4096 rows whole sequences lie end to end from the first row, each row holding its position in its sequence (0, 1, 2, ...); rows after the last sequence hold -1. Some fsdp index holds one sequence of 4096 rows and some has unused rows. In every fsdp index one sequence covers rows 2047 and 2048.
All inputs are finite; a program needn't handle non-finite values.
Results may differ from the reference program's by a relative error of at most 0.02.
Values may be sent and summed in bfloat16 or wider, within the bound.
No kernel may reach another device: no remote copies, remote signals or barrier semaphores. Data moves between devices by JAX's collectives and lax.ppermute only.
A program may use at most 192 MiB of HBM per device.

```python
from functools import partial
import jax
import jax.numpy as jnp
from jax import lax

D = 1024
HEADS = 32
HEADDIM = 64
STATE = 128
CONV = 4
STRETCH = 256
TOK_DEV = 2048
INNER = 2048
GROUP = 4096
TOKENS = 16384
N_FSDP = 4
N_CTX = 2


def draw_positions(key, part):
    key = jax.random.fold_in(key, 7)
    key_used, key_starts, key_full, key_short = jax.random.split(key, 4)
    slot_index = jnp.arange(GROUP)
    group_index = jnp.arange(N_FSDP)
    full_group = jax.random.randint(key_full, (), 0, N_FSDP)
    short_group = (full_group + 1 + jax.random.randint(key_short, (), 0, N_FSDP - 1)) % N_FSDP
    lowest = (N_CTX - 1) * TOK_DEV + 1
    used_rows = jax.random.randint(key_used, (N_FSDP,), lowest, GROUP + 1)
    used_rows = jnp.where(group_index == full_group, GROUP, jnp.where(group_index == short_group, lowest, used_rows))
    start_odds = max(GROUP // 6, 2)
    starts = jax.random.randint(key_starts, (N_FSDP, GROUP), 0, start_odds) == 0
    middle = (slot_index > TOK_DEV - 1) & (slot_index <= (N_CTX - 1) * TOK_DEV)
    starts = starts & (slot_index[None, :] < used_rows[:, None]) & jnp.logical_not(middle)[None, :] & (group_index != full_group)[:, None]
    starts = starts | (slot_index == 0)[None, :]
    last_start = lax.cummax(jnp.where(starts, slot_index[None, :], 0), axis=1)
    positions = jnp.where(slot_index[None, :] < used_rows[:, None], slot_index[None, :] - last_start, -1)
    return positions.reshape(N_FSDP * GROUP).astype(jnp.int32)


def block_levels(rng, dims, shards, low, top_value):
    def one(axis_at, shards_of):
        steps = jax.random.uniform(jax.random.fold_in(jax.random.fold_in(rng, 6), axis_at), (shards_of,), jnp.float32, low / len(shards), top_value / len(shards))
        return jnp.repeat(jnp.exp(steps), dims[axis_at] // shards_of).reshape((-1,) + (1,) * (len(dims) - axis_at - 1))

    factor_of = one(*shards[0])
    for cut in shards[1:]:
        factor_of = factor_of * one(*cut)
    return factor_of


def normal_values(own_key, extent, width, bound, shards=(), held_as=jnp.bfloat16):
    array = jax.random.normal(own_key, extent, jnp.float32) * width
    if len(shards) > 0:
        array = block_levels(own_key, extent, shards, -0.22, 0.18) * array
    return jnp.clip(array, min=-bound, max=bound).astype(held_as)


def setup_inputs(seed: int = 0) -> dict:
    key_list = jax.random.split(jax.random.key(seed), 15)
    tokens = normal_values(key_list[0], (TOKENS, D), 1.0, 6.0, ((0, 8),))
    norm_gain = jnp.clip(1.0 + 0.1 * jax.random.normal(key_list[1], (D,), jnp.float32), 0.5, 1.5).astype(jnp.bfloat16)
    inner_weight = normal_values(key_list[2], (2, D, INNER), D ** -0.5, 0.1875, ((1, 8), (2, 4)))
    state_weight = normal_values(key_list[3], (D, 2 * STATE), D ** -0.5, 0.1875, ((0, 8),))
    step_weight = normal_values(key_list[4], (D, HEADS), D ** -0.5, 0.1875, ((0, 8), (1, 4)))
    inner_taps = normal_values(key_list[5], (CONV + 1, INNER), CONV ** -0.5, 3.0, ((1, 4),), jnp.float32)
    state_taps = normal_values(key_list[6], (CONV + 1, 2 * STATE), CONV ** -0.5, 3.0, (), jnp.float32)
    step_bias = jnp.clip(-4.0 + 3.0 * jax.random.uniform(key_list[7], (HEADS,), jnp.float32) ** block_levels(key_list[7], (HEADS,), ((0, 4),), -0.2, 0.2), -4.0, -1.0)
    log_rate = jnp.clip(-2.5 + 4.0 * jax.random.uniform(key_list[8], (HEADS,), jnp.float32) ** block_levels(key_list[8], (HEADS,), ((0, 4),), -0.2, 0.2), -2.5, 1.5)
    skip_gain = jnp.clip(0.5 + 1.0 * jax.random.uniform(key_list[9], (HEADS,), jnp.float32) ** block_levels(key_list[9], (HEADS,), ((0, 4),), -0.2, 0.2), 0.5, 1.5)
    gated_gain = jnp.clip(1.0 + 0.1 * jax.random.normal(key_list[10], (INNER,), jnp.float32), 0.5, 1.5)
    out_weight = normal_values(key_list[11], (INNER, D), INNER ** -0.5, 0.125, ((0, 4), (1, 8)))
    out_grad = normal_values(key_list[12], (TOKENS, D), 1.0, 6.0, ((0, 8),))
    positions = draw_positions(jax.random.fold_in(key_list[14], 71), 0)
    return {"tokens": tokens, "norm_gain": norm_gain, "inner_weight": inner_weight, "state_weight": state_weight, "step_weight": step_weight, "inner_taps": inner_taps, "state_taps": state_taps, "step_bias": step_bias, "log_rate": log_rate, "skip_gain": skip_gain, "gated_gain": gated_gain, "out_weight": out_weight, "out_grad": out_grad, "positions": positions}


epsilon = 1e-05
highest = lax.Precision.HIGHEST

@jax.custom_vjp
def low(v):
    return lax.optimization_barrier(v.astype(jnp.bfloat16)).astype(jnp.float32)

@jax.custom_vjp
def low_back(v):
    return v

def low_keep(v):
    return (low(v), None)

def low_pass(kept, grad):
    return (grad,)

def back_keep(v):
    return (v, None)

def back_low(kept, grad):
    return (low(grad),)
low.defvjp(low_keep, low_pass)
low_back.defvjp(back_keep, back_low)

def causal_taps(mixed_in, conv_taps, positions):
    row_count = mixed_in.shape[0]
    summed = conv_taps[CONV][None, :] + conv_taps[CONV - 1][None, :] * mixed_in
    for offset in range(1, CONV):
        shifted = jnp.concatenate([jnp.zeros((offset, mixed_in.shape[1]), jnp.float32), mixed_in[:row_count - offset]], axis=0)
        inside = (positions >= offset).astype(jnp.float32)[:, None]
        summed = summed + conv_taps[CONV - 1 - offset][None, :] * shifted * inside
    return summed

def stretch_block(carried, pieces, skip_gain, decay_rate):
    values, state_keys, state_queries, steps_dt, positions = pieces
    stretch_width = positions.shape[0]
    places = jnp.arange(stretch_width)
    log_decay = jnp.cumsum(steps_dt * decay_rate[None, :], axis=0)
    same_seq = (places[None, :] <= places[:, None]) & (places[:, None] - places[None, :] <= positions[:, None])
    gram_matrix = low_back(jnp.dot(state_queries, state_keys.T, precision=highest))
    log_spans = log_decay[:, None, :] - log_decay[None, :, :]
    decays = jnp.where(same_seq[:, :, None], jnp.exp(jnp.where(same_seq[:, :, None], log_spans, 0.0)), 0.0)
    mixing = low(gram_matrix[:, :, None] * decays * steps_dt[None, :, :])
    within = jnp.einsum('ijh,jhp->ihp', mixing, values, precision=highest)
    entering = (positions >= places + 1).astype(jnp.float32)[:, None] * jnp.exp(log_decay)
    across = entering[:, :, None] * jnp.einsum('in,hpn->ihp', state_queries, carried, precision=highest)
    output = within + across + skip_gain[None, :, None] * values
    ending = (places >= stretch_width - 1 - positions[stretch_width - 1]).astype(jnp.float32)
    weight_end = ending[:, None] * jnp.exp(log_decay[stretch_width - 1][None, :] - log_decay) * steps_dt
    fresh_state = jnp.einsum('jh,jhp,jn->hpn', weight_end, values, state_keys, precision=highest)
    passing = (positions[stretch_width - 1] >= stretch_width).astype(jnp.float32) * jnp.exp(log_decay[stretch_width - 1])
    return (passing[:, None, None] * carried + fresh_state, output)

def group_forward(tok_float, positions, params):
    norm_gain, inner_weight, state_weight, step_weight, inner_taps, state_taps, step_bias, log_rate, skip_gain, gated_gain, out_weight = params
    valid_rows = (positions >= 0).astype(jnp.float32)
    scaling = lax.rsqrt(lax.optimization_barrier(jnp.mean(tok_float * tok_float, axis=-1, keepdims=True)) + epsilon)
    normed = low(tok_float * scaling * norm_gain[None, :])
    gate_pre = low_back(jnp.dot(normed, inner_weight[0], precision=highest))
    inner_in = jnp.dot(normed, inner_weight[1], precision=highest)
    state_in = jnp.dot(normed, state_weight, precision=highest)
    step_raw = jnp.dot(normed, step_weight, precision=highest)
    mixed_in = low_back(low(jnp.concatenate([inner_in, state_in], axis=1)))
    conv_taps = jnp.concatenate([inner_taps, state_taps], axis=1)
    convolved = jax.nn.silu(causal_taps(mixed_in, conv_taps, positions))
    values = low(convolved[:, :INNER])
    state_keys = low(convolved[:, INNER:INNER + STATE])
    state_queries = low(convolved[:, INNER + STATE:])
    steps_dt = jax.nn.softplus(step_raw + step_bias[None, :]) * valid_rows[:, None]
    decay_rate = -jnp.exp(log_rate)
    stretch_count = GROUP // STRETCH
    pieces = (values.reshape(stretch_count, STRETCH, HEADS, HEADDIM), state_keys.reshape(stretch_count, STRETCH, STATE), state_queries.reshape(stretch_count, STRETCH, STATE), steps_dt.reshape(stretch_count, STRETCH, HEADS), positions.reshape(stretch_count, STRETCH))
    stretch_step = jax.checkpoint(partial(stretch_block, skip_gain=skip_gain, decay_rate=decay_rate))
    _, outputs = lax.scan(stretch_step, jnp.zeros((HEADS, HEADDIM, STATE), jnp.float32), pieces)
    ssm_out = low_back(outputs.reshape(GROUP, INNER))
    gated = ssm_out * jax.nn.silu(gate_pre)
    gated_scale = lax.rsqrt(lax.optimization_barrier(jnp.mean(gated * gated, axis=-1, keepdims=True)) + epsilon)
    normed_out = low(gated * gated_scale * gated_gain[None, :] * valid_rows[:, None])
    return tok_float + jnp.dot(normed_out, out_weight, precision=highest)

def whole_layer(tok_all, params, pos_all):
    group_fn = jax.checkpoint(partial(group_forward, params=params))

    def per_group(unused_carry, group_items):
        return (unused_carry, group_fn(group_items[0], group_items[1]))
    _, results = lax.scan(per_group, jnp.zeros((), jnp.float32), (tok_all, pos_all))
    return results

def reference(tokens, norm_gain, inner_weight, state_weight, step_weight, inner_taps, state_taps, step_bias, log_rate, skip_gain, gated_gain, out_weight, out_grad, positions):
    params = tuple((member.astype(jnp.float32) for member in (norm_gain, inner_weight, state_weight, step_weight, inner_taps, state_taps, step_bias, log_rate, skip_gain, gated_gain, out_weight)))
    tok_all = tokens.astype(jnp.float32).reshape(N_FSDP, GROUP, D)
    pos_all = positions.reshape(N_FSDP, GROUP)
    forward = partial(whole_layer, pos_all=pos_all)
    result, pullback = jax.vjp(forward, tok_all, params)
    tok_grad, param_grads = pullback(out_grad.astype(jnp.float32).reshape(N_FSDP, GROUP, D))
    return (result.reshape(TOKENS, D).astype(jnp.bfloat16), tok_grad.reshape(TOKENS, D), param_grads[0], param_grads[1], param_grads[2], param_grads[3], param_grads[4], param_grads[5], param_grads[6], param_grads[7], param_grads[8], param_grads[9], param_grads[10])
```

```python
import functools

import jax
import jax.numpy as jnp
from jax import lax
from jax.experimental import pallas as pl
from jax.experimental.pallas import tpu as pltpu
from jax.sharding import PartitionSpec as P

CONV = 4
STRETCH = 256
INNER = 2048
LANES = 128
HALO = 16
NEVER = -1e30
VMEM_BYTES = 60 * 1024 * 1024

epsilon = 1e-05
bf16 = jnp.bfloat16
f32 = jnp.float32


def swap_ctx(x):
    return lax.ppermute(x, "ctx", [(0, 1), (1, 0)])


def swap_fsdp(x, k):
    return lax.ppermute(x, "fsdp", [(i, i ^ k) for i in range(4)])


def swap_tp(x, k):
    return lax.ppermute(x, "tp", [(i, i ^ k) for i in range(4)])


def row_shares():
    return 2 if small_mesh() and lax.axis_size("tp") == 4 else 1


def shift_part(x, by):
    tp, shares = lax.axis_size("tp"), row_shares()
    parts, group = lax.axis_size("ctx") * shares, tp // shares

    def device(part, k):
        return part // shares * tp + part % shares * group + k

    pairs = [
        (device(part, k), device(part + by, k))
        for part in range(parts)
        if 0 <= part + by < parts
        for k in range(group)
    ]
    return lax.ppermute(x, ("ctx", "tp"), pairs)


def small_mesh():
    return lax.axis_size("fsdp") == 4 and lax.axis_size("ctx") == 2


def gather_near(x):
    if not small_mesh():
        return [lax.all_gather(x, ("fsdp", "ctx"), axis=0, tiled=True)]
    return [x] + [swap_fsdp(x, k) for k in (1, 2, 3)]


def gather_stacks(near):
    stack = jnp.stack(near)
    return [stack, swap_ctx(stack)] if small_mesh() else [stack]


def gather_place(size):
    if not small_mesh():
        return jnp.zeros((1,), jnp.int32)
    me = lax.axis_index("fsdp")
    core = lax.axis_index("ctx")
    place = [(me ^ k) * 2 + core for k in range(4)] + [(me ^ k) * 2 + 1 - core for k in range(4)]
    return (jnp.stack(place) * size).astype(jnp.int32)


def scatter_rows(x):
    if not small_mesh():
        x = x.reshape(-1, x.shape[-1])
        return lax.psum_scatter(x, ("fsdp", "ctx"), scatter_dimension=0, tiled=True).astype(f32)
    me = lax.axis_index("fsdp")
    core = lax.axis_index("ctx")
    theirs = swap_ctx(lax.dynamic_index_in_dim(x, 1 - core, 0, False))
    mine = lax.dynamic_index_in_dim(x, core, 0, False)
    summed = (mine.astype(f32) + theirs.astype(f32)).astype(bf16)
    total = lax.dynamic_index_in_dim(summed, me, 0, False).astype(f32)
    for k in (1, 2, 3):
        total = total + swap_fsdp(lax.dynamic_index_in_dim(summed, me ^ k, 0, False), k).astype(f32)
    return total


def sum_rows_group(x):
    if not small_mesh():
        return lax.psum(x, ("fsdp", "ctx"))
    x = x + swap_ctx(x)
    x = x + swap_fsdp(x, 1)
    return x + swap_fsdp(x, 2)


def sum_tp_small(x):
    if lax.axis_size("tp") != 4:
        return lax.psum(x, "tp").astype(f32)
    pair = (x.astype(f32) + swap_tp(x, 1).astype(f32)).astype(x.dtype)
    return pair.astype(f32) + swap_tp(pair, 2).astype(f32)


def tied(x, *others):
    return lax.optimization_barrier((x,) + others)[0]


def nn(a, b):
    return jnp.dot(a, b, preferred_element_type=f32)


def nt(a, b):
    return lax.dot_general(a, b, (((1,), (1,)), ((), ())), preferred_element_type=f32)


def tn(a, b):
    return lax.dot_general(a, b, (((0,), (0,)), ((), ())), preferred_element_type=f32)


def two_terms(x):
    high = x.astype(bf16)
    return high, (x - high.astype(f32)).astype(bf16)


def dot_pair(x, choice):
    high, low = two_terms(x)
    return nn(high, choice) + nn(low, choice)


def dot_triple(choice, x):
    high = x.astype(bf16)
    rest = x - high.astype(f32)
    middle, low = two_terms(rest)
    return nn(choice, high) + nn(choice, middle) + nn(choice, low)


def iota(shape, axis):
    return lax.broadcasted_iota(jnp.int32, shape, axis)


def head_choice(channels, head_size):
    return (iota((LANES, channels), 1) // head_size == iota((LANES, channels), 0)).astype(bf16)


def head_choice_t(channels, head_size):
    return (iota((channels, LANES), 0) // head_size == iota((channels, LANES), 1)).astype(bf16)


def head_column(row, choice_t):
    return jnp.sum(choice_t.astype(f32) * row, axis=1, keepdims=True)


def column(rows):
    if rows.shape[0] == 1:
        return jnp.broadcast_to(rows, (LANES, STRETCH)).T
    return jnp.concatenate([rows, jnp.zeros((LANES - rows.shape[0], STRETCH), f32)], axis=0).T


def row_norm(rows):
    scaling = lax.rsqrt(jnp.mean(rows * rows, axis=-1, keepdims=True) + epsilon)
    return scaling, rows * scaling


def softplus(v):
    return jnp.maximum(v, 0.0) + jnp.log1p(jnp.exp(-jnp.abs(v)))


def pair_sel(x, part, head_size):
    return jnp.where(iota(x.shape, 1) // head_size == part, x, jnp.zeros_like(x))


def mask_matrix(pos):
    wide = jnp.concatenate([pos] * (STRETCH // LANES), axis=1)
    ahead = (iota((STRETCH, STRETCH), 0) - iota((STRETCH, STRETCH), 1)).astype(f32)
    return jnp.where((ahead >= 0.0) & (ahead <= wide), 0.0, NEVER)


def carry_factor(pos, decay):
    places = iota((STRETCH, LANES), 0).astype(f32)
    return jnp.where(pos >= places + 1.0, jnp.exp(decay), 0.0)


def passing_row(pos, decay):
    last = slice(STRETCH - 1, STRETCH)
    return jnp.where(pos[last] >= float(STRETCH), jnp.exp(decay[last]), 0.0)


def pack_state(ref, state, through, own_heads):
    channels = state.shape[0]
    ref[:channels, :] = state.astype(bf16)
    row, col = iota((LANES, LANES), 0), iota((LANES, LANES), 1)
    turn = (row < 2 * own_heads) & (
        jnp.where(row < own_heads, row + own_heads, row - own_heads) == col
    )
    low = jnp.broadcast_to(through, (8, LANES))
    turned = dot_pair(low, turn.astype(bf16))
    ref[channels:, :] = jnp.concatenate([low, turned], axis=0).astype(bf16)


def join_states(refs, choice_t, groups):
    channels = choice_t.shape[0]
    half = channels // 2
    total = None
    for distance in range(len(refs), 0, -1):
        ref = refs[distance - 1]
        state = ref[:channels, :].astype(f32)
        through = ref[channels:, :].astype(f32)
        if groups == 2 and distance % 2 == 1:
            state = jnp.concatenate([state[half:], state[:half]], axis=0)
            through = through[8:9]
        else:
            through = through[0:1]
        total = state if total is None else state + head_column(through, choice_t) * total
    return total


def end_factor(pos, decay):
    last = slice(STRETCH - 1, STRETCH)
    places = iota((STRETCH, LANES), 0).astype(f32)
    return jnp.where(places >= STRETCH - 1.0 - pos[last], jnp.exp(decay[last] - decay), 0.0)


def steps_of(step_pre, pos, heads):
    lanes = iota((STRETCH, LANES), 1)
    return jnp.where((lanes < heads) & (pos >= 0.0), softplus(step_pre), 0.0)


def conv_of(mx_ref, taps_ref, pos):
    total = taps_ref[CONV : CONV + 1, :] + taps_ref[CONV - 1 : CONV, :] * mx_ref[8 : 8 + STRETCH, :]
    for s in range(1, CONV):
        window = mx_ref[8 - s : 8 - s + STRETCH, :] * (pos[:, :1] >= float(s)).astype(f32)
        total = total + taps_ref[CONV - 1 - s : CONV - s, :] * window
    return total


def place_stacks(place_ref, stacks, write):
    number = 0
    for stack in stacks:
        size = stack.shape[1]
        for k in range(stack.shape[0]):
            write(pl.ds(pl.multiple_of(place_ref[number], size), size), stack[k])
            number += 1


def forward_kernel(dims, count, groups, place_ref, *refs):
    own_stacks, refs = refs[:count], refs[count:]
    more_stacks, refs = refs[: count * (groups - 1)], refs[count * (groups - 1) :]
    pos_ref, tok_ref, halo_ref, taps_ref, bias_ref, rate_ref, skip_ref = refs[:7]
    gate_ref, mixed_ref, vkq_ref, ssm_ref, step_ref, decay_ref, enter_ref, last_ref = refs[7:15]
    edge_ref, gain_ref, w_ref, mx, state, through = refs[15:]
    heads, head_size, inner, states = dims
    width = inner + 2 * states
    at_mixed, at_misc = inner, inner + width
    c = pl.program_id(0)

    @pl.when(c == 0)
    def _():
        own = inner // groups

        def write_own(at, piece):
            w_ref[at, 0:own] = piece[:, 0:own]
            w_ref[at, at_mixed : at_mixed + own] = piece[:, own : 2 * own]
            w_ref[at, at_mixed + inner : at_misc] = piece[:, 2 * own : 2 * own + 2 * states]
            w_ref[at, at_misc:] = piece[:, 2 * own + 2 * states :]

        def write_more(at, piece):
            w_ref[at, own:inner] = piece[:, 0:own]
            w_ref[at, at_mixed + own : at_mixed + inner] = piece[:, own : 2 * own]
            w_ref[at, at_misc:] = w_ref[at, at_misc:] + piece[:, 2 * own :]

        place_stacks(place_ref, own_stacks, write_own)
        place_stacks(place_ref, more_stacks, write_more)
        misc = w_ref[:, at_misc:].astype(f32).T
        gain_ref[...] = jnp.broadcast_to(misc[heads : heads + 1], gain_ref.shape)
        unit = row_norm(halo_ref[...].astype(f32))[1]
        low = (unit * gain_ref[0:1, :]).astype(bf16)
        edge = nn(low, w_ref[:, at_mixed:at_misc]).astype(bf16)
        edge_ref[...] = edge
        mx[0:8, :] = edge[HALO - 8 :].astype(f32)
        state[...] = jnp.zeros_like(state)
        through[...] = jnp.ones_like(through)

    @pl.when(c > 0)
    def _():
        mx[0:8, :] = mx[STRETCH : STRETCH + 8, :]

    pos = column(pos_ref[0].astype(f32))
    unit = row_norm(tok_ref[...].astype(f32))[1]
    normed = (unit * gain_ref[0:1, :]).astype(bf16)
    gate_ref[...] = nn(normed, w_ref[:, :at_mixed])
    mixed = nn(normed, w_ref[:, at_mixed:at_misc]).astype(bf16)
    mixed_ref[...] = mixed
    mx[8 : 8 + STRETCH, :] = mixed.astype(f32)
    step_pre = nn(normed, w_ref[:, at_misc:]) + bias_ref[...]
    step_ref[...] = step_pre
    conv = conv_of(mx, taps_ref, pos)
    vkq = (conv * jax.nn.sigmoid(conv)).astype(bf16)
    vkq_ref[...] = vkq
    values, keys, queries = vkq[:, :inner], vkq[:, inner : inner + states], vkq[:, inner + states :]
    dt = steps_of(step_pre, pos, heads)
    rate = -jnp.exp(rate_ref[...])
    tri = (iota((STRETCH, STRETCH), 1) <= iota((STRETCH, STRETCH), 0)).astype(bf16)
    decay = dot_triple(tri, dt * rate)
    decay_ref[...] = decay
    decay_t = decay.T
    mask = mask_matrix(pos)
    gram = nt(queries, keys)
    choice = head_choice(inner, head_size)
    value_f = values.astype(f32)
    dt_values = (value_f * dot_pair(dt, choice)).astype(bf16)
    per = LANES // head_size
    within = []
    for pair in range(inner // LANES):
        part = dt_values[:, pair * LANES : (pair + 1) * LANES]
        total = None
        for k in range(per):
            h = pair * per + k
            m = (gram * jnp.exp((decay[:, h : h + 1] - decay_t[h : h + 1, :]) + mask)).astype(bf16)
            term = nn(m, pair_sel(part, k, head_size))
            total = term if total is None else total + term
        within.append(total)
    within = jnp.concatenate(within, axis=1)
    entering = state[...]
    enter_ref[0] = entering
    across = nt(queries, entering.astype(bf16)) * dot_pair(carry_factor(pos, decay), choice)
    ssm_ref[...] = within + across + skip_ref[...] * value_f
    wend = end_factor(pos, decay) * dt
    fresh = tn((value_f * dot_pair(wend, choice)).astype(bf16), keys)
    passing = passing_row(pos, decay)
    through[...] = through[...] * passing
    state[...] = head_column(passing, head_choice_t(inner, head_size)) * entering + fresh

    @pl.when(c == pl.num_programs(0) - 1)
    def _():
        pack_state(last_ref, state[...], through[0:1, :], heads // groups)


def stats_kernel(dims, count, groups, hops, place_ref, *refs):
    stacks, refs = refs[:count], refs[count:]
    come_refs, refs = refs[:hops], refs[hops:]
    pos_ref, ssm_ref, gate_ref, q_ref, decay_ref, enter_ref, og_ref, gain_ref = refs[:8]
    full_ref, state_ref, gno_ref, stats_ref, branch_ref, out_ref, through, come = refs[8:]
    heads, head_size, inner, states = dims
    c = pl.program_id(0)

    @pl.when(c == 0)
    def _():
        def write(at, piece):
            out_ref[at, :] = piece

        place_stacks(place_ref, stacks, write)
        through[...] = jnp.ones_like(through)
        come[...] = join_states(come_refs, head_choice_t(inner, head_size), groups)

    pos = column(pos_ref[0].astype(f32))
    decay = decay_ref[...]
    coming = come[...]
    choice = head_choice(inner, head_size)
    before = through[0:1, :]
    state_ref[0] = (
        enter_ref[0] + head_column(before, head_choice_t(inner, head_size)) * coming
    ).astype(bf16)
    across = nt(q_ref[...], coming.astype(bf16))
    ssm = ssm_ref[...] + across * dot_pair(carry_factor(pos, decay) * before, choice)
    full_ref[...] = ssm
    through[...] = through[...] * passing_row(pos, decay)
    gate = gate_ref[...]
    gated = ssm * (gate * jax.nn.sigmoid(gate))
    gno = nn(og_ref[...], out_ref[...])
    gno_ref[...] = gno
    gain = gain_ref[...] * (pos[:, :1] >= 0.0).astype(f32)
    branch_ref[...] = nt((gated * gain).astype(bf16), out_ref[...]).astype(bf16)
    grad_unit = gno * gain
    squares = jnp.sum(gated * gated, axis=1, keepdims=True)
    dots = jnp.sum(grad_unit * gated, axis=1, keepdims=True)
    lanes = iota((STRETCH, LANES), 1)
    stats_ref[...] = jnp.where(lanes == 0, squares, dots).T[0:2]


def gate_back_kernel(
    dims, groups,
    pos_ref, stats_ref, ssm_ref, gate_ref, gno_ref, vkq_ref, decay_ref, gain_ref, skip_ref,
    gssm_ref, ggate_ref, low_ref, glog_ref, leave_ref, last_ref, sums_ref,
    back, through,
):
    heads, head_size, inner, states = dims
    step = pl.program_id(0)

    @pl.when(step == 0)
    def _():
        back[...] = jnp.zeros_like(back)
        through[...] = jnp.ones_like(through)
        sums_ref[...] = jnp.zeros_like(sums_ref)

    pos = column(pos_ref[0].astype(f32))
    valid = (pos[:, :1] >= 0.0).astype(f32)
    stats = column(stats_ref[...])
    scale = lax.rsqrt(stats[:, 0:1] / INNER + epsilon)
    dots = stats[:, 1:2]
    gate = gate_ref[...]
    ssm = ssm_ref[...]
    sig = jax.nn.sigmoid(gate)
    act = gate * sig
    gated = ssm * act
    unit = gated * scale
    gain = gain_ref[...]
    gno = gno_ref[...]
    low_ref[...] = (unit * gain * valid).astype(bf16)
    grad_unit = gno * gain * valid
    grad_gated = scale * (grad_unit - gated * (scale * scale * dots * (1.0 / INNER)))
    gssm = (grad_gated * act).astype(bf16)
    gssm_ref[...] = gssm
    ggate_ref[...] = (grad_gated * ssm * sig * (1.0 + gate * (1.0 - sig))).astype(bf16)
    g = gssm.astype(f32)
    value_f = vkq_ref[:, :inner].astype(f32)
    queries = vkq_ref[:, inner + states :]
    g_values = g * value_f
    choice = head_choice(inner, head_size)
    choice_t = head_choice_t(inner, head_size)
    glog_ref[...] = dot_pair(g * ssm - skip_ref[...] * g_values, choice_t)
    sums_ref[0:1, :] += jnp.sum(gno * unit * valid, axis=0, keepdims=True)
    sums_ref[1:2, :] += jnp.sum(g_values, axis=0, keepdims=True)
    decay = decay_ref[...]
    core = (g * dot_pair(carry_factor(pos, decay), choice)).astype(bf16)
    after = back[...]
    leave_ref[0] = after
    passing = passing_row(pos, decay)
    through[...] = through[...] * passing
    back[...] = tn(core, queries) + head_column(passing, choice_t) * after

    @pl.when(step == pl.num_programs(0) - 1)
    def _():
        pack_state(last_ref, back[...], through[0:1, :], heads // groups)


def scan_back_kernel(
    dims, first, blocks, groups, hops,
    pos_ref, tok_ref, w_ref, gain_ref, taps_ref, rate_ref, skip_ref, mixed_ref, before_ref,
    edge_ref, vkq_ref, gssm_ref, ggate_ref, glog_ref, step_ref, decay_ref, state_ref, leave_ref,
    gp_in, pp_in, suffix_in, gsum_in, tsum_in, hsum_in, *refs,
):
    go_refs, refs = refs[:hops], refs[hops:]
    part_ref, ret_ref, grads_ref, gp_out, pp_out, suffix, gsum_ref, tsum_ref, hsum_ref = refs[-14:-5]
    mx, gp, pp, edge, go = refs[-5:]
    heads, head_size, inner, states = dims
    width = inner + 2 * states
    at_mixed, at_misc = inner, inner + width
    step = pl.program_id(0)
    c = blocks - 1 - first - step

    @pl.when(step == 0)
    def _():
        for out, given in (
            (suffix, suffix_in), (gsum_ref, gsum_in), (tsum_ref, tsum_in), (hsum_ref, hsum_in)
        ):
            out[...] = given[...]
        go[...] = join_states(go_refs, head_choice_t(inner, head_size), groups)
        gp[STRETCH : STRETCH + 8, :] = gp_in[...]
        pp[STRETCH : STRETCH + 8, :] = pp_in[...]

    @pl.when(step > 0)
    def _():
        gp[STRETCH : STRETCH + 8, :] = gp[0:8, :]
        pp[STRETCH : STRETCH + 8, :] = pp[0:8, :]

    @pl.when(c == 0)
    def _():
        mx[0:8, :] = edge_ref[HALO - 8 :, :].astype(f32)

    @pl.when(c > 0)
    def _():
        mx[0:8, :] = before_ref[HALO - 8 :, :].astype(f32)

    pos = column(pos_ref[0].astype(f32))
    pp[0:STRETCH, :] = pos
    mx[8 : 8 + STRETCH, :] = mixed_ref[...].astype(f32)
    values = vkq_ref[:, :inner]
    keys = vkq_ref[:, inner : inner + states]
    queries = vkq_ref[:, inner + states :]
    value_f = values.astype(f32)
    gssm = gssm_ref[...]
    g = gssm.astype(f32)
    step_pre = step_ref[...]
    decay = decay_ref[...]
    decay_t = decay.T
    dt = steps_of(step_pre, pos, heads)
    rate = -jnp.exp(rate_ref[...])
    choice = head_choice(inner, head_size)
    choice_t = head_choice_t(inner, head_size)
    dt_wide = dot_pair(dt, choice)
    dt_values = (value_f * dt_wide).astype(bf16)
    mask = mask_matrix(pos)
    gram = nt(queries, keys)
    per = LANES // head_size
    grad_gram = None
    turned = []
    for pair in range(inner // LANES):
        lanes = slice(pair * LANES, (pair + 1) * LANES)
        total = None
        for k in range(per):
            h = pair * per + k
            spread = jnp.exp((decay[:, h : h + 1] - decay_t[h : h + 1, :]) + mask)
            own_g = pair_sel(gssm[:, lanes], k, head_size)
            term = tn((gram * spread).astype(bf16), own_g)
            total = term if total is None else total + term
            more = nt(own_g, dt_values[:, lanes]) * spread
            grad_gram = more if grad_gram is None else grad_gram + more
        turned.append(total)
    turned = jnp.concatenate(turned, axis=1)
    grad_gram = grad_gram.astype(bf16)
    entering = state_ref[0]
    after = suffix[0:1, :]
    leaving = leave_ref[0] + head_column(after, choice_t) * go[...]
    leaving_low = leaving.astype(bf16)
    passing = passing_row(pos, decay)
    suffix[...] = suffix[...] * passing
    far = end_factor(pos, decay)
    wend = far * dt
    wend_wide = dot_pair(wend, choice)
    keyed = nt(keys, leaving_low)
    core = (g * dot_pair(carry_factor(pos, decay), choice)).astype(bf16)
    grad_values = skip_ref[...] * g + dt_wide * turned + wend_wide * keyed
    grad_keys = tn(grad_gram, queries) + nn((value_f * wend_wide).astype(bf16), leaving_low)
    grad_queries = nn(grad_gram, keys) + nn(core, entering)
    within_dt = dot_pair(value_f * turned, choice_t)
    within_logs = dot_pair(dt_values.astype(f32) * turned, choice_t)
    grad_wend = dot_pair(value_f * keyed, choice_t)
    through = jnp.sum(leaving * entering.astype(f32), axis=1, keepdims=True)
    last_grad = passing * jnp.sum(through * choice_t.astype(f32), axis=0, keepdims=True)
    end_terms = grad_wend * wend
    grad_logs = glog_ref[...] - within_logs - end_terms
    at_last = iota((STRETCH, LANES), 0) == STRETCH - 1
    grad_logs = grad_logs + jnp.where(
        at_last, jnp.sum(end_terms, axis=0, keepdims=True) + last_grad, 0.0
    )
    tri = (iota((STRETCH, STRETCH), 1) >= iota((STRETCH, STRETCH), 0)).astype(bf16)
    grad_steps = dot_triple(tri, grad_logs)
    grad_dt = within_dt + grad_wend * far + grad_steps * rate
    lane_ok = (iota((STRETCH, LANES), 1) < heads) & (pos >= 0.0)
    grad_step = jnp.where(lane_ok, grad_dt * jax.nn.sigmoid(step_pre), 0.0)
    hsum_ref[0:1, :] += jnp.sum(grad_step, axis=0, keepdims=True)
    hsum_ref[1:2, :] += jnp.sum(grad_steps * dt, axis=0, keepdims=True) * rate

    conv = conv_of(mx, taps_ref, pos)
    sig = jax.nn.sigmoid(conv)
    grad_conv = jnp.concatenate([grad_values, grad_keys, grad_queries], axis=1)
    grad_pre = grad_conv * (sig * (1.0 + conv * (1.0 - sig)))
    gp[0:STRETCH, :] = grad_pre
    tsum_ref[CONV : CONV + 1, :] += jnp.sum(grad_pre, axis=0, keepdims=True)
    tsum_ref[CONV - 1 : CONV, :] += jnp.sum(
        grad_pre * mx[8 : 8 + STRETCH, :], axis=0, keepdims=True
    )
    grad_mixed = grad_pre * taps_ref[CONV - 1 : CONV, :]
    for s in range(1, CONV):
        inside = (pos[:, :1] >= float(s)).astype(f32)
        tsum_ref[CONV - 1 - s : CONV - s, :] += jnp.sum(
            grad_pre * inside * mx[8 - s : 8 - s + STRETCH, :], axis=0, keepdims=True
        )
        later = (pp[s : s + STRETCH, :][:, :1] >= float(s)).astype(f32)
        grad_mixed = grad_mixed + gp[s : s + STRETCH, :] * later * taps_ref[
            CONV - 1 - s : CONV - s, :
        ]
    grads = jnp.concatenate(
        [ggate_ref[...], grad_mixed.astype(bf16), grad_step.astype(bf16)], axis=1
    )
    partial = nt(grads, w_ref[...])
    unit = row_norm(tok_ref[...].astype(f32))[1]
    grads_ref[...] = grads[:, at_mixed:]
    gp_out[...] = gp[0:8, :]
    pp_out[...] = pp[0:8, :]
    part_ref[...] = partial.astype(bf16)
    gsum_ref[0:1, :] += jnp.sum(partial * unit, axis=0, keepdims=True)
    ret_ref[...] = jnp.zeros_like(ret_ref)

    @pl.when(c == 0)
    def _():
        edge[0:8, :] = jnp.zeros((8, width), f32)
        total = jnp.zeros((8, width), f32)
        for s in range(1, CONV):
            inside = (pos[0:8, :1] >= float(s)).astype(f32)
            edge[8:16, :] = gp[0:8, :] * inside
            total = total + edge[s : s + 8, :] * taps_ref[CONV - 1 - s : CONV - s, :]
        ret_ref[...] = total


def spread_rows(out_ref, total_ref, groups, cores):
    size = total_ref.shape[0] // (cores * groups)
    for at in range(cores * groups):
        out_ref[at % cores, at // cores] = total_ref[at * size : (at + 1) * size, :].astype(bf16)


def first_grad_kernel(
    dims, groups, cores, tok_ref, gain_ref, gate_ref, og_ref, low_ref, out_ref, total
):
    inner = dims[2]
    c = pl.program_id(0)

    @pl.when(c == 0)
    def _():
        total[...] = jnp.zeros_like(total)

    normed = (row_norm(tok_ref[...].astype(f32))[1] * gain_ref[0:1, :]).astype(bf16)
    total[:, :inner] += tn(normed, gate_ref[...])
    total[:, inner:] += tn(og_ref[...], low_ref[...])

    @pl.when(c == pl.num_programs(0) - 1)
    def _():
        spread_rows(out_ref, total, groups, cores)


def weight_grad_kernel(
    dims, groups, cores,
    tok_ref, gain_ref, grads_ref, extra_ref, gsum_ref, tail_ref,
    out_ref,
    total,
):
    heads, head_size, inner, states = dims
    width = inner + 2 * states
    c = pl.program_id(0)

    @pl.when(c == 0)
    def _():
        total[...] = jnp.zeros_like(total)

    unit = row_norm(tok_ref[...].astype(f32))[1]
    normed = (unit * gain_ref[0:1, :]).astype(bf16)
    total[...] += tn(normed, grads_ref[...])

    @pl.when(c == pl.num_programs(0) - 1)
    def _():
        total[:, :width] += tn(normed[STRETCH - HALO :], extra_ref[...])
        norm = gsum_ref[0:1, :] + jnp.sum(
            tail_ref[...] * unit[STRETCH - HALO :], axis=0, keepdims=True
        )
        norm = jnp.broadcast_to(norm, (LANES, norm.shape[1])).T
        misc = total[:, width:]
        total[:, width:] = jnp.where(iota(misc.shape, 1) == heads, norm, misc)
        spread_rows(out_ref, total, groups, cores)


def mixed_out_kernel(stats_ref, branch_ref, tok_ref, out_ref):
    scale = lax.rsqrt(column(stats_ref[...])[:, 0:1] / INNER + epsilon)
    out_ref[...] = (tok_ref[...].astype(f32) + scale * branch_ref[...].astype(f32)).astype(bf16)


def tokens_grad_kernel(grad_ref, tok_ref, og_ref, gain_ref, out_ref):
    scaling, unit = row_norm(tok_ref[...].astype(f32))
    grad = grad_ref[...].astype(f32) * gain_ref[0:1, :]
    mean = jnp.mean(grad * unit, axis=-1, keepdims=True)
    out_ref[...] = scaling * (grad - unit * mean) + og_ref[...].astype(f32)


def own_rows_kernel(mine_ref, came_ref, tok_ref, gain_ref, tail_ref, out_ref):
    scaling, unit = row_norm(tok_ref[...].astype(f32))
    grad = mine_ref[...].astype(f32) + came_ref[...].astype(f32)
    size, model = grad.shape
    tail = jnp.concatenate([jnp.zeros((size - HALO, model), f32), tail_ref[...]], axis=0)
    grad = grad + jnp.where(pl.program_id(0) == pl.num_programs(0) - 1, tail, 0.0)
    grad = grad * gain_ref[0:1, :]
    mean = jnp.mean(grad * unit, axis=-1, keepdims=True)
    out_ref[...] = (scaling * (grad - unit * mean)).astype(bf16)


def add_kernel(a_ref, b_ref, out_ref):
    out_ref[...] = a_ref[...].astype(f32) + b_ref[...].astype(f32)


def own_branch_kernel(stats_ref, mine_ref, came_ref, tok_ref, out_ref):
    scale = lax.rsqrt(column(stats_ref[...])[:, 0:1] / INNER + epsilon)
    branch = mine_ref[...].astype(f32) + came_ref[...].astype(f32)
    out_ref[...] = (tok_ref[...].astype(f32) + scale * branch).astype(bf16)


def per_device(
    tokens,
    norm_gain,
    inner_weight,
    state_weight,
    step_weight,
    inner_taps,
    state_taps,
    step_bias,
    log_rate,
    skip_gain,
    gated_gain,
    out_weight,
    out_grad,
    positions,
):
    shares = row_shares()
    share = lax.axis_index("tp") // (lax.axis_size("tp") // shares)
    all_rows, model = tokens.shape
    rows = all_rows // shares
    own_heads = step_bias.shape[0]
    own_inner = gated_gain.shape[0]
    head_size = own_inner // own_heads
    heads, inner = own_heads * shares, own_inner * shares
    states = state_weight.shape[1] // 2
    blocks = rows // STRETCH
    width = inner + 2 * states
    at_mixed, at_misc = inner, inner + width
    columns = at_misc + LANES
    dims = (heads, head_size, inner, states)
    parts = lax.axis_size("ctx") * shares

    def own_share(x, size):
        return x if shares == 1 else lax.dynamic_slice_in_dim(x, share * size, size)

    def joined(groups, begin, size):
        return [g[:, begin : begin + size] for g in groups]

    def steps_at(lane):
        return jnp.pad(step_weight, ((0, 0), (lane, LANES - lane - own_heads)))

    own_rows_of = norm_gain.shape[0]
    gain_lanes = jnp.concatenate(
        [
            jnp.zeros((own_rows_of, heads), bf16),
            norm_gain[:, None],
            jnp.zeros((own_rows_of, LANES - heads - 1), bf16),
        ],
        axis=1,
    )
    edge_rows = lax.ppermute(tokens[all_rows - HALO :], "ctx", [(0, 1)])
    all_tokens, all_grad = tokens, out_grad
    tokens, out_grad = own_share(tokens, rows), own_share(out_grad, rows)
    positions = own_share(positions, rows)
    halo_tokens = edge_rows
    if shares > 1:
        halo_tokens = jnp.where(share == 0, edge_rows, all_tokens[rows - HALO : rows])

    head_params = jnp.stack([step_bias, log_rate, skip_gain])
    small_own = jnp.concatenate(
        [
            jnp.pad(jnp.concatenate([inner_taps, gated_gain[None]]), ((0, 8 - CONV - 2), (0, 0))),
            jnp.pad(head_params, ((0, 5), (0, LANES - own_heads))),
        ],
        axis=1,
    )
    channels_in = [inner_weight[0], inner_weight[1]]
    near = gather_near(
        jnp.concatenate(channels_in + [state_weight, steps_at(0) + gain_lanes], axis=1)
    )
    stacks = gather_stacks(near)
    count = len(stacks)
    out_near = out_weight.T
    if shares > 1:
        more = swap_tp(jnp.concatenate(channels_in + [steps_at(own_heads)], axis=1), 2)
        near = gather_near(tied(more, tokens, out_grad, halo_tokens))
        out_more = swap_tp(tied(out_near, more), 2)
        small_more = swap_tp(tied(small_own, more), 2)
        near[-1] = tied(near[-1], out_more, small_more)
        stacks += gather_stacks(near)
        out_near = jnp.concatenate([out_near, out_more], axis=1)
    out_near = gather_near(tied(out_near, near[-1]))
    place = gather_place(own_rows_of)

    small_groups = [small_own] + ([small_more] if shares > 1 else [])
    channel_rows = jnp.concatenate(joined(small_groups, 0, own_inner), axis=1)
    head_rows = jnp.concatenate(joined(small_groups, own_inner, own_heads), axis=1)
    taps = jnp.concatenate(
        [channel_rows, jnp.pad(state_taps, ((0, 8 - CONV - 1), (0, 0)))], axis=1
    )
    gain_row = channel_rows[CONV + 1 : CONV + 2]
    skip_row = jnp.repeat(head_rows[2], head_size)[None, :]
    head_rows = jnp.pad(head_rows, ((0, 0), (0, LANES - heads)))
    bias_row, rate_row = head_rows[0:1], head_rows[1:2]
    pos_rows = positions.reshape(blocks, 1, STRETCH)

    def fixed(shape):
        return pl.BlockSpec(shape, lambda c: (0,) * len(shape))

    def by_rows(cols, order, at=0):
        return pl.BlockSpec((STRETCH, cols), lambda c: (order(c), at))

    def by_block(order):
        return pl.BlockSpec((1, inner, states), lambda c: (order(c), 0, 0))

    def pos_spec(order):
        return pl.BlockSpec((1, 1, STRETCH), lambda c: (order(c), 0, 0))

    def ahead(c):
        return c

    def reverse(c):
        return blocks - 1 - c

    def shape(*dims_of, dtype=f32):
        return jax.ShapeDtypeStruct(dims_of, dtype)

    light = pl.CostEstimate(flops=1024, bytes_accessed=1024, transcendentals=0)
    params = pltpu.CompilerParams(
        dimension_semantics=("arbitrary",), vmem_limit_bytes=VMEM_BYTES
    )

    scalars = pl.BlockSpec(memory_space=pltpu.SMEM)
    gate, mixed, vkq, ssm_local, step_pre, decay, enter, last_state, edge, model_gain, weight = (
        pl.pallas_call(
            functools.partial(forward_kernel, dims, count, shares),
            grid=(blocks,),
            in_specs=[
                scalars,
                *[fixed(a.shape) for a in stacks],
                pos_spec(ahead),
                by_rows(model, ahead),
                fixed((HALO, model)),
                fixed((8, width)),
                fixed((1, LANES)),
                fixed((1, LANES)),
                fixed((1, inner)),
            ],
            out_specs=[
                by_rows(inner, ahead),
                by_rows(width, ahead),
                by_rows(width, ahead),
                by_rows(inner, ahead),
                by_rows(LANES, ahead),
                by_rows(LANES, ahead),
                by_block(ahead),
                fixed((inner + HALO, states)),
                fixed((HALO, width)),
                fixed((8, model)),
                fixed((model, columns)),
            ],
            out_shape=[
                shape(rows, inner),
                shape(rows, width, dtype=bf16),
                shape(rows, width, dtype=bf16),
                shape(rows, inner),
                shape(rows, LANES),
                shape(rows, LANES),
                shape(blocks, inner, states),
                shape(inner + HALO, states, dtype=bf16),
                shape(HALO, width, dtype=bf16),
                shape(8, model),
                shape(model, columns, dtype=bf16),
            ],
            scratch_shapes=[
                pltpu.VMEM((STRETCH + 8, width), f32),
                pltpu.VMEM((inner, states), f32),
                pltpu.VMEM((8, LANES), f32),
            ],
            compiler_params=params,
            name="forward",
        )(
            place, *stacks, pos_rows, tokens, halo_tokens, taps, bias_row, rate_row, skip_row
        )
    )
    out_stacks = gather_stacks(out_near[:-1] + [tied(out_near[-1], last_state)])
    coming = [shift_part(last_state, by) for by in range(1, parts)]
    ssm, state, grad_out, stats, branch, out_t = pl.pallas_call(
        functools.partial(stats_kernel, dims, count, shares, parts - 1),
        grid=(blocks,),
        in_specs=[
            scalars,
            *[fixed(a.shape) for a in out_stacks],
            *[fixed((inner + HALO, states))] * (parts - 1),
            pos_spec(ahead),
            by_rows(inner, ahead),
            by_rows(inner, ahead),
            by_rows(states, ahead, (inner + states) // states),
            by_rows(LANES, ahead),
            by_block(ahead),
            by_rows(model, ahead),
            fixed((1, inner)),
        ],
        out_specs=[
            by_rows(inner, ahead),
            by_block(ahead),
            by_rows(inner, ahead),
            pl.BlockSpec((2, STRETCH), lambda c: (0, c)),
            by_rows(model, ahead),
            fixed((model, inner)),
        ],
        out_shape=[
            shape(rows, inner),
            shape(blocks, inner, states, dtype=bf16),
            shape(rows, inner),
            shape(2, rows),
            shape(rows, model, dtype=bf16),
            shape(model, inner, dtype=bf16),
        ],
        scratch_shapes=[pltpu.VMEM((8, LANES), f32), pltpu.VMEM((inner, states), f32)],
        compiler_params=params,
        name="stats",
    )(
        place, *out_stacks, *coming, pos_rows, ssm_local, gate, vkq, decay, enter, out_grad, gain_row
    )
    half = rows // 2
    member = lax.axis_index("tp") % 2

    def halves(x):
        sent = lax.dynamic_slice_in_dim(x, (1 - member) * half, half)
        return lax.dynamic_slice_in_dim(tied(x, sent), member * half, half), swap_tp(sent, 1)

    if shares > 1:
        own_tokens = lax.dynamic_slice_in_dim(tokens, member * half, half)
        stats = stats + swap_tp(stats, 1)
        own_branch = pl.pallas_call(
            own_branch_kernel,
            grid=(half // STRETCH,),
            in_specs=[pl.BlockSpec((2, STRETCH), lambda c: (0, c))]
            + [by_rows(model, ahead)] * 3,
            out_specs=by_rows(model, ahead),
            out_shape=shape(half, model, dtype=bf16),
            compiler_params=params,
            name="own_branch",
        )(
            lax.dynamic_slice_in_dim(stats, member * half, half, 1),
            *halves(tied(branch, stats)),
            own_tokens,
        )
    else:
        stats = sum_tp_small(stats)
        first_total = lax.psum(branch, "tp")
    grad_ssm, grad_gate, normed_out, grad_logs, leave, last_back, gate_sums = pl.pallas_call(
        functools.partial(gate_back_kernel, dims, shares),
        grid=(blocks,),
        in_specs=[
            pos_spec(reverse),
            pl.BlockSpec((2, STRETCH), lambda c: (0, reverse(c))),
            by_rows(inner, reverse),
            by_rows(inner, reverse),
            by_rows(inner, reverse),
            by_rows(width, reverse),
            by_rows(LANES, reverse),
            fixed((1, inner)),
            fixed((1, inner)),
        ],
        out_specs=[
            by_rows(inner, reverse),
            by_rows(inner, reverse),
            by_rows(inner, reverse),
            by_rows(LANES, reverse),
            by_block(reverse),
            fixed((inner + HALO, states)),
            fixed((8, inner)),
        ],
        out_shape=[
            shape(rows, inner, dtype=bf16),
            shape(rows, inner, dtype=bf16),
            shape(rows, inner, dtype=bf16),
            shape(rows, LANES),
            shape(blocks, inner, states),
            shape(inner + HALO, states, dtype=bf16),
            shape(8, inner),
        ],
        scratch_shapes=[pltpu.VMEM((inner, states), f32), pltpu.VMEM((8, LANES), f32)],
        compiler_params=params,
        cost_estimate=light,
        name="gate_back",
    )(pos_rows, stats, ssm, gate, grad_out, vkq, decay, gain_row, skip_row)
    going = [shift_part(last_back, -by) for by in range(1, parts)]
    if shares > 1:
        mixed_out = lax.all_gather(tied(own_branch, *going), "tp", axis=0, tiled=True)
        first_total = mixed_out[:8, :LANES]
    near_count, cores = (lax.axis_size("fsdp"), lax.axis_size("ctx")) if small_mesh() else (1, 1)

    def grad_shape(cols):
        return (cores, near_count, model // (cores * near_count), cols)

    first_grad = pl.pallas_call(
        functools.partial(first_grad_kernel, dims, near_count, cores),
        grid=(blocks,),
        in_specs=[
            by_rows(model, ahead),
            fixed((8, model)),
            by_rows(inner, ahead),
            by_rows(model, ahead),
            by_rows(inner, ahead),
        ],
        out_specs=fixed(grad_shape(2 * inner)),
        out_shape=shape(*grad_shape(2 * inner), dtype=bf16),
        scratch_shapes=[pltpu.VMEM((model, 2 * inner), f32)],
        compiler_params=params,
        cost_estimate=light,
        name="first_grad",
    )(tokens, model_gain, grad_gate, out_grad, normed_out)
    grad_gate = tied(grad_gate, first_grad)
    first_grad = scatter_rows(first_grad)
    per_halo = STRETCH // HALO

    def scan_piece(first, size, going, carried):
        def place_of(c):
            return blocks - 1 - first - c

        grads_before, *carried = carried
        carry_shapes = [a.shape for a in carried]
        aliases = {}
        in_specs = [
            pos_spec(place_of),
            by_rows(model, place_of),
            fixed((model, columns)),
            fixed((8, model)),
            fixed((8, width)),
            fixed((1, LANES)),
            fixed((1, inner)),
            by_rows(width, place_of),
            pl.BlockSpec(
                (HALO, width), lambda c: (jnp.maximum(place_of(c) * per_halo - 1, 0), 0)
            ),
            fixed((HALO, width)),
            by_rows(width, place_of),
            by_rows(inner, place_of),
            by_rows(inner, place_of),
            by_rows(LANES, place_of),
            by_rows(LANES, place_of),
            by_rows(LANES, place_of),
            by_block(place_of),
            by_block(place_of),
            *[fixed(a) for a in carry_shapes],
            *[fixed((inner + HALO, states))] * (parts - 1),
        ]
        operands = [
            pos_rows, tokens, weight, model_gain, taps, rate_row, skip_row, mixed, mixed, edge,
            vkq, grad_ssm, grad_gate, grad_logs, step_pre, decay, state, leave, *carried, *going,
        ]
        if grads_before is not None:
            aliases = {len(operands): 2}
            operands.append(grads_before)
            in_specs.append(pl.BlockSpec(memory_space=pl.ANY))
        return pl.pallas_call(
            functools.partial(scan_back_kernel, dims, first, blocks, shares, parts - 1),
            grid=(size,),
            in_specs=in_specs,
            out_specs=[
                pl.BlockSpec((STRETCH, model), lambda c: (size - 1 - c, 0)),
                fixed((8, width)),
                by_rows(columns - inner, place_of),
                *[fixed(a) for a in carry_shapes],
            ],
            out_shape=[
                shape(size * STRETCH, model, dtype=bf16),
                shape(8, width),
                shape(rows, columns - inner, dtype=bf16),
                *[shape(*a) for a in carry_shapes],
            ],
            input_output_aliases=aliases,
            scratch_shapes=[
                pltpu.VMEM((STRETCH + 8, width), f32),
                pltpu.VMEM((STRETCH + 8, width), f32),
                pltpu.VMEM((STRETCH + 8, LANES), f32),
                pltpu.VMEM((16, width), f32),
                pltpu.VMEM((inner, states), f32),
            ],
            compiler_params=params,
            cost_estimate=light,
        name="scan_back",
        )(*operands)

    carried = [
        None,
        jnp.zeros((8, width), f32),
        jnp.zeros((8, LANES), f32),
        jnp.ones((8, LANES), f32),
        jnp.zeros((8, model), f32),
        jnp.zeros((8, width), f32),
        jnp.zeros((8, LANES), f32),
    ]
    partial, returned, *carried = scan_piece(0, blocks, going, carried)
    grads, _, _, _, norm_sums, tap_sums, head_sums = carried

    small = jnp.concatenate([tap_sums.reshape(-1, LANES), gate_sums.reshape(-1, LANES), head_sums])
    if shares > 1:
        mine, came = halves(partial)
        small = tied(small, mine)
    small = sum_rows_group(small)
    extra = shift_part(returned, -1).astype(bf16)
    if shares > 1:
        extra = jnp.concatenate(
            [extra[:, own_inner:inner], extra[:, :own_inner], extra[:, inner:]], axis=1
        )
    extra = jnp.concatenate([jnp.zeros((HALO - 8, width), bf16), extra], axis=0)
    tail_part = nt(extra, weight[:, at_mixed:at_misc])

    if shares > 1:
        tail_low = tail_part.astype(bf16)
        tail_sum = tail_low.astype(f32) + swap_tp(tail_low, 1).astype(f32)
        tail_sum = jnp.where(member == 1, tail_sum, 0.0)
        own_rows = pl.pallas_call(
            own_rows_kernel,
            grid=(half // STRETCH,),
            in_specs=[by_rows(model, ahead)] * 3 + [fixed((8, model)), fixed((HALO, model))],
            out_specs=by_rows(model, ahead),
            out_shape=shape(half, model, dtype=bf16),
            compiler_params=params,
            name="own_rows",
        )(tied(mine, first_grad), came, own_tokens, model_gain, tail_sum)
        grads = tied(grads, own_rows, small, first_total)
        own_rows = tied(own_rows, first_total)
        second_total = lax.all_gather(own_rows, "tp", axis=0, tiled=True)
    else:
        partial = partial.at[rows - HALO :].add(tail_part.astype(bf16))
        partial = tied(partial, first_total)
        mixed_out = pl.pallas_call(
            mixed_out_kernel,
            grid=(blocks,),
            in_specs=[
                pl.BlockSpec((2, STRETCH), lambda c: (0, c)),
                by_rows(model, ahead),
                by_rows(model, ahead),
            ],
            out_specs=by_rows(model, ahead),
            out_shape=shape(rows, model, dtype=bf16),
            compiler_params=params,
            name="mixed_out",
        )(stats, first_total, tokens)
        tokens_grad = pl.pallas_call(
            tokens_grad_kernel,
            grid=(blocks,),
            in_specs=[by_rows(model, ahead)] * 3 + [fixed((8, model))],
            out_specs=by_rows(model, ahead),
            out_shape=shape(rows, model),
            compiler_params=params,
            name="tokens_grad",
        )(lax.psum(partial, "tp"), tokens, out_grad, model_gain)

    weight_grad = pl.pallas_call(
        functools.partial(weight_grad_kernel, dims, near_count, cores),
        grid=(blocks,),
        in_specs=[
            by_rows(model, ahead),
            fixed((8, model)),
            by_rows(columns - inner, ahead),
            fixed((HALO, width)),
            fixed((8, model)),
            fixed((HALO, model)),
        ],
        out_specs=fixed(grad_shape(columns - inner)),
        out_shape=shape(*grad_shape(columns - inner), dtype=bf16),
        scratch_shapes=[pltpu.VMEM((model, columns - inner), f32)],
        compiler_params=params,
        cost_estimate=light,
        name="weight_grad",
    )(tokens, model_gain, grads, extra, norm_sums, tail_part)
    late_grad = scatter_rows(weight_grad)
    at = 8 * width // LANES
    tap_total = small[:at].reshape(8, width)
    gate_total = small[at : at + 8 * inner // LANES].reshape(8, inner)
    head_total = small[at + 8 * inner // LANES :]
    shared = late_grad[:, inner:].astype(bf16)
    state_taps_grad = tap_total[: CONV + 1, inner:]
    rows_of = jnp.concatenate([tap_total[: CONV + 1, :inner], gate_total[:2]])
    channels_of = [first_grad[:, :inner], late_grad[:, :inner], first_grad[:, inner:]]
    steps_of_grad = late_grad[:, width:]
    groups = [g[:, :own_inner] for g in channels_of] + [steps_of_grad[:, :own_heads]]
    channel_total, head_total = rows_of[:, :own_inner], head_total[:2, :LANES]
    if shares > 1:
        sent = [g[:, own_inner:] for g in channels_of]
        sent.append(steps_of_grad[:, own_heads:])
        sent.append(jnp.zeros((steps_of_grad.shape[0], own_heads), f32))
        sent = jnp.concatenate(sent, axis=1).astype(bf16)
        few = jnp.concatenate(
            [
                jnp.pad(rows_of[:, own_inner:], ((0, 1), (0, 0))),
                jnp.pad(
                    head_total[:, own_heads : own_heads + LANES // 2], ((0, 6), (0, LANES // 2))
                ),
            ],
            axis=1,
        )
        pair = (shared.astype(f32) + swap_tp(shared, 1).astype(f32)).astype(bf16)
        taps_pair = state_taps_grad + swap_tp(state_taps_grad, 1)
        came, few = swap_tp(sent, 2).astype(f32), swap_tp(few, 2)
        groups = [
            g + came[:, k * own_inner : k * own_inner + g.shape[1]] for k, g in enumerate(groups)
        ]
        channel_total = channel_total + few[: CONV + 3, :own_inner]
        head_total = head_total[:, :own_heads] + few[:2, own_inner : own_inner + own_heads]
        shared = pair.astype(f32) + swap_tp(pair, 2).astype(f32)
        state_taps_grad = taps_pair + swap_tp(taps_pair, 2)
    else:
        shared = sum_tp_small(shared)
        state_taps_grad = sum_tp_small(state_taps_grad)
        head_total = head_total[:, :own_heads]
    state_weight_grad = shared[:, : 2 * states]
    norm_gain_grad = shared[:, 2 * states + heads]
    inner_weight_grad = jnp.stack(groups[:2])
    out_weight_grad = groups[2].T
    if shares > 1:
        second_total = tied(second_total, inner_weight_grad, out_weight_grad)
        tokens_grad = pl.pallas_call(
            add_kernel,
            grid=(all_rows // STRETCH,),
            in_specs=[by_rows(model, ahead)] * 2,
            out_specs=by_rows(model, ahead),
            out_shape=shape(all_rows, model),
            compiler_params=params,
            name="tokens_grad",
        )(second_total, all_grad)
    return (
        mixed_out,
        tokens_grad,
        norm_gain_grad,
        inner_weight_grad,
        state_weight_grad,
        groups[3],
        channel_total[: CONV + 1],
        state_taps_grad,
        head_total[0],
        head_total[1],
        jnp.sum(channel_total[CONV + 2].reshape(own_heads, head_size), axis=1),
        channel_total[CONV + 1],
        out_weight_grad,
    )


def solution(mesh):
    return jax.shard_map(
        per_device,
        mesh=mesh,
        in_specs=(
            P(("fsdp", "ctx"), None),
            P(("fsdp", "ctx")),
            P(None, ("fsdp", "ctx"), "tp"),
            P(("fsdp", "ctx"), None),
            P(("fsdp", "ctx"), "tp"),
            P(None, "tp"),
            P(),
            P("tp"),
            P("tp"),
            P("tp"),
            P("tp"),
            P("tp", ("fsdp", "ctx")),
            P(("fsdp", "ctx"), None),
            P(("fsdp", "ctx")),
        ),
        out_specs=(
            P(("fsdp", "ctx"), None),
            P(("fsdp", "ctx"), None),
            P(("fsdp", "ctx")),
            P(None, ("fsdp", "ctx"), "tp"),
            P(("fsdp", "ctx"), None),
            P(("fsdp", "ctx"), "tp"),
            P(None, "tp"),
            P(),
            P("tp"),
            P("tp"),
            P("tp"),
            P("tp"),
            P("tp", ("fsdp", "ctx")),
        ),
        check_vma=False,
    )
```

```python
import functools

import jax
import jax.numpy as jnp
from jax import lax
from jax.experimental import pallas as pl
from jax.experimental.pallas import tpu as pltpu
from jax.sharding import PartitionSpec as P

CONV = 4
STRETCH = 256
INNER = 2048
LANES = 128
HALO = 16
NEVER = -1e30
VMEM_BYTES = 60 * 1024 * 1024

epsilon = 1e-05
bf16 = jnp.bfloat16
f32 = jnp.float32


def swap_ctx(x):
    return lax.ppermute(x, "ctx", [(0, 1), (1, 0)])


def swap_fsdp(x, k):
    return lax.ppermute(x, "fsdp", [(i, i ^ k) for i in range(4)])


def swap_tp(x, k):
    return lax.ppermute(x, "tp", [(i, i ^ k) for i in range(4)])


def row_shares():
    return 2 if small_mesh() and lax.axis_size("tp") == 4 else 1


def shift_part(x, by):
    tp, shares = lax.axis_size("tp"), row_shares()
    parts, group = lax.axis_size("ctx") * shares, tp // shares

    def device(part, k):
        return part // shares * tp + part % shares * group + k

    pairs = [
        (device(part, k), device(part + by, k))
        for part in range(parts)
        if 0 <= part + by < parts
        for k in range(group)
    ]
    return lax.ppermute(x, ("ctx", "tp"), pairs)


def small_mesh():
    return lax.axis_size("fsdp") == 4 and lax.axis_size("ctx") == 2


def gather_near(x):
    if not small_mesh():
        return [lax.all_gather(x, ("fsdp", "ctx"), axis=0, tiled=True)]
    return [x] + [swap_fsdp(x, k) for k in (1, 2, 3)]


def gather_stacks(near):
    stack = jnp.stack(near)
    return [stack, swap_ctx(stack)] if small_mesh() else [stack]


def gather_place(size):
    if not small_mesh():
        return jnp.zeros((1,), jnp.int32)
    me = lax.axis_index("fsdp")
    core = lax.axis_index("ctx")
    place = [(me ^ k) * 2 + core for k in range(4)] + [(me ^ k) * 2 + 1 - core for k in range(4)]
    return (jnp.stack(place) * size).astype(jnp.int32)


def scatter_rows(x):
    if not small_mesh():
        x = x.reshape(-1, x.shape[-1])
        return lax.psum_scatter(x, ("fsdp", "ctx"), scatter_dimension=0, tiled=True).astype(f32)
    me = lax.axis_index("fsdp")
    core = lax.axis_index("ctx")
    theirs = swap_ctx(lax.dynamic_index_in_dim(x, 1 - core, 0, False))
    mine = lax.dynamic_index_in_dim(x, core, 0, False)
    summed = (mine.astype(f32) + theirs.astype(f32)).astype(bf16)
    total = lax.dynamic_index_in_dim(summed, me, 0, False).astype(f32)
    for k in (1, 2, 3):
        total = total + swap_fsdp(lax.dynamic_index_in_dim(summed, me ^ k, 0, False), k).astype(f32)
    return total


def sum_rows_group(x):
    if not small_mesh():
        return lax.psum(x, ("fsdp", "ctx"))
    x = x + swap_ctx(x)
    x = x + swap_fsdp(x, 1)
    return x + swap_fsdp(x, 2)


def sum_tp_small(x):
    if lax.axis_size("tp") != 4:
        return lax.psum(x, "tp").astype(f32)
    pair = (x.astype(f32) + swap_tp(x, 1).astype(f32)).astype(x.dtype)
    return pair.astype(f32) + swap_tp(pair, 2).astype(f32)


def tied(x, *others):
    return lax.optimization_barrier((x,) + others)[0]


def nn(a, b):
    return jnp.dot(a, b, preferred_element_type=f32)


def nt(a, b):
    return lax.dot_general(a, b, (((1,), (1,)), ((), ())), preferred_element_type=f32)


def tn(a, b):
    return lax.dot_general(a, b, (((0,), (0,)), ((), ())), preferred_element_type=f32)


def two_terms(x):
    high = x.astype(bf16)
    return high, (x - high.astype(f32)).astype(bf16)


def dot_pair(x, choice):
    high, low = two_terms(x)
    return nn(high, choice) + nn(low, choice)


def dot_triple(choice, x):
    high = x.astype(bf16)
    rest = x - high.astype(f32)
    middle, low = two_terms(rest)
    return nn(choice, high) + nn(choice, middle) + nn(choice, low)


def iota(shape, axis):
    return lax.broadcasted_iota(jnp.int32, shape, axis)


def head_choice(channels, head_size):
    return (iota((LANES, channels), 1) // head_size == iota((LANES, channels), 0)).astype(bf16)


def head_choice_t(channels, head_size):
    return (iota((channels, LANES), 0) // head_size == iota((channels, LANES), 1)).astype(bf16)


def head_column(row, choice_t):
    return jnp.sum(choice_t.astype(f32) * row, axis=1, keepdims=True)


def column(rows):
    if rows.shape[0] == 1:
        return jnp.broadcast_to(rows, (LANES, STRETCH)).T
    return jnp.concatenate([rows, jnp.zeros((LANES - rows.shape[0], STRETCH), f32)], axis=0).T


def row_norm(rows):
    scaling = lax.rsqrt(jnp.mean(rows * rows, axis=-1, keepdims=True) + epsilon)
    return scaling, rows * scaling


def softplus(v):
    return jnp.maximum(v, 0.0) + jnp.log1p(jnp.exp(-jnp.abs(v)))


def pair_sel(x, part, head_size):
    return jnp.where(iota(x.shape, 1) // head_size == part, x, jnp.zeros_like(x))


def mask_matrix(pos):
    wide = jnp.concatenate([pos] * (STRETCH // LANES), axis=1)
    ahead = (iota((STRETCH, STRETCH), 0) - iota((STRETCH, STRETCH), 1)).astype(f32)
    return jnp.where((ahead >= 0.0) & (ahead <= wide), 0.0, NEVER)


def carry_factor(pos, decay):
    places = iota((STRETCH, LANES), 0).astype(f32)
    return jnp.where(pos >= places + 1.0, jnp.exp(decay), 0.0)


def passing_row(pos, decay):
    last = slice(STRETCH - 1, STRETCH)
    return jnp.where(pos[last] >= float(STRETCH), jnp.exp(decay[last]), 0.0)


def pack_state(ref, state, through, own_heads):
    channels = state.shape[0]
    ref[:channels, :] = state.astype(bf16)
    row, col = iota((LANES, LANES), 0), iota((LANES, LANES), 1)
    turn = (row < 2 * own_heads) & (
        jnp.where(row < own_heads, row + own_heads, row - own_heads) == col
    )
    low = jnp.broadcast_to(through, (8, LANES))
    turned = dot_pair(low, turn.astype(bf16))
    ref[channels:, :] = jnp.concatenate([low, turned], axis=0).astype(bf16)


def join_states(refs, choice_t, groups):
    channels = choice_t.shape[0]
    half = channels // 2
    total = None
    for distance in range(len(refs), 0, -1):
        ref = refs[distance - 1]
        state = ref[:channels, :].astype(f32)
        through = ref[channels:, :].astype(f32)
        if groups == 2 and distance % 2 == 1:
            state = jnp.concatenate([state[half:], state[:half]], axis=0)
            through = through[8:9]
        else:
            through = through[0:1]
        total = state if total is None else state + head_column(through, choice_t) * total
    return total


def end_factor(pos, decay):
    last = slice(STRETCH - 1, STRETCH)
    places = iota((STRETCH, LANES), 0).astype(f32)
    return jnp.where(places >= STRETCH - 1.0 - pos[last], jnp.exp(decay[last] - decay), 0.0)


def steps_of(step_pre, pos, heads):
    lanes = iota((STRETCH, LANES), 1)
    return jnp.where((lanes < heads) & (pos >= 0.0), softplus(step_pre), 0.0)


def conv_of(mx_ref, taps_ref, pos):
    total = taps_ref[CONV : CONV + 1, :] + taps_ref[CONV - 1 : CONV, :] * mx_ref[8 : 8 + STRETCH, :]
    for s in range(1, CONV):
        window = mx_ref[8 - s : 8 - s + STRETCH, :] * (pos[:, :1] >= float(s)).astype(f32)
        total = total + taps_ref[CONV - 1 - s : CONV - s, :] * window
    return total


def place_stacks(place_ref, stacks, write):
    number = 0
    for stack in stacks:
        size = stack.shape[1]
        for k in range(stack.shape[0]):
            write(pl.ds(pl.multiple_of(place_ref[number], size), size), stack[k])
            number += 1


def forward_kernel(dims, count, groups, place_ref, *refs):
    own_stacks, refs = refs[:count], refs[count:]
    more_stacks, refs = refs[: count * (groups - 1)], refs[count * (groups - 1) :]
    pos_ref, tok_ref, halo_ref, taps_ref, bias_ref, rate_ref, skip_ref = refs[:7]
    mixed_ref, vkq_ref, ssm_ref, step_ref, decay_ref, enter_ref, last_ref = refs[7:14]
    edge_ref, gain_ref, w_ref, mx, state, through = refs[14:]
    heads, head_size, inner, states = dims
    width = inner + 2 * states
    at_mixed, at_misc = inner, inner + width
    c = pl.program_id(0)

    @pl.when(c == 0)
    def _():
        own = inner // groups

        def write_own(at, piece):
            w_ref[at, 0:own] = piece[:, 0:own]
            w_ref[at, at_mixed : at_mixed + own] = piece[:, own : 2 * own]
            w_ref[at, at_mixed + inner : at_misc] = piece[:, 2 * own : 2 * own + 2 * states]
            w_ref[at, at_misc:] = piece[:, 2 * own + 2 * states :]

        def write_more(at, piece):
            w_ref[at, own:inner] = piece[:, 0:own]
            w_ref[at, at_mixed + own : at_mixed + inner] = piece[:, own : 2 * own]
            w_ref[at, at_misc:] = w_ref[at, at_misc:] + piece[:, 2 * own :]

        place_stacks(place_ref, own_stacks, write_own)
        place_stacks(place_ref, more_stacks, write_more)
        misc = w_ref[:, at_misc:].astype(f32).T
        gain_ref[...] = jnp.broadcast_to(misc[heads : heads + 1], gain_ref.shape)
        unit = row_norm(halo_ref[...].astype(f32))[1]
        low = (unit * gain_ref[0:1, :]).astype(bf16)
        edge = nn(low, w_ref[:, at_mixed:at_misc]).astype(bf16)
        edge_ref[...] = edge
        mx[0:8, :] = edge[HALO - 8 :].astype(f32)
        state[...] = jnp.zeros_like(state)
        through[...] = jnp.ones_like(through)

    @pl.when(c > 0)
    def _():
        mx[0:8, :] = mx[STRETCH : STRETCH + 8, :]

    pos = column(pos_ref[0].astype(f32))
    unit = row_norm(tok_ref[...].astype(f32))[1]
    normed = (unit * gain_ref[0:1, :]).astype(bf16)
    mixed = nn(normed, w_ref[:, at_mixed:at_misc]).astype(bf16)
    mixed_ref[...] = mixed
    mx[8 : 8 + STRETCH, :] = mixed.astype(f32)
    step_pre = nn(normed, w_ref[:, at_misc:]) + bias_ref[...]
    step_ref[...] = step_pre
    conv = conv_of(mx, taps_ref, pos)
    vkq = (conv * jax.nn.sigmoid(conv)).astype(bf16)
    vkq_ref[...] = vkq
    values, keys, queries = vkq[:, :inner], vkq[:, inner : inner + states], vkq[:, inner + states :]
    dt = steps_of(step_pre, pos, heads)
    rate = -jnp.exp(rate_ref[...])
    tri = (iota((STRETCH, STRETCH), 1) <= iota((STRETCH, STRETCH), 0)).astype(bf16)
    decay = dot_triple(tri, dt * rate)
    decay_ref[...] = decay
    decay_t = decay.T
    mask = mask_matrix(pos)
    gram = nt(queries, keys)
    choice = head_choice(inner, head_size)
    value_f = values.astype(f32)
    dt_values = (value_f * dot_pair(dt, choice)).astype(bf16)
    per = LANES // head_size
    within = []
    for pair in range(inner // LANES):
        part = dt_values[:, pair * LANES : (pair + 1) * LANES]
        total = None
        for k in range(per):
            h = pair * per + k
            m = (gram * jnp.exp((decay[:, h : h + 1] - decay_t[h : h + 1, :]) + mask)).astype(bf16)
            term = nn(m, pair_sel(part, k, head_size))
            total = term if total is None else total + term
        within.append(total)
    within = jnp.concatenate(within, axis=1)
    entering = state[...]
    enter_ref[0] = entering
    across = nt(queries, entering.astype(bf16)) * dot_pair(carry_factor(pos, decay), choice)
    ssm_ref[...] = within + across + skip_ref[...] * value_f
    wend = end_factor(pos, decay) * dt
    fresh = tn((value_f * dot_pair(wend, choice)).astype(bf16), keys)
    passing = passing_row(pos, decay)
    through[...] = through[...] * passing
    state[...] = head_column(passing, head_choice_t(inner, head_size)) * entering + fresh

    @pl.when(c == pl.num_programs(0) - 1)
    def _():
        pack_state(last_ref, state[...], through[0:1, :], heads // groups)


def gates_kernel(count, place_ref, *refs):
    stacks, refs = refs[:count], refs[count:]
    tok_ref, gain_ref, w_ref, og_ref, gate_ref, gno_ref, out_ref = refs

    @pl.when(pl.program_id(0) == 0)
    def _():
        def write(at, piece):
            out_ref[at, :] = piece

        place_stacks(place_ref, stacks, write)

    normed = (row_norm(tok_ref[...].astype(f32))[1] * gain_ref[0:1, :]).astype(bf16)
    gate_ref[...] = nn(normed, w_ref[...])
    gno_ref[...] = nn(og_ref[...], out_ref[...])


def stats_kernel(dims, groups, hops, *refs):
    come_refs, refs = refs[:hops], refs[hops:]
    pos_ref, ssm_ref, gate_ref, q_ref, decay_ref, enter_ref, gno_ref, out_ref, gain_ref = refs[:9]
    full_ref, state_ref, stats_ref, branch_ref, through, come = refs[9:]
    heads, head_size, inner, states = dims
    c = pl.program_id(0)

    @pl.when(c == 0)
    def _():
        through[...] = jnp.ones_like(through)
        come[...] = join_states(come_refs, head_choice_t(inner, head_size), groups)

    pos = column(pos_ref[0].astype(f32))
    decay = decay_ref[...]
    coming = come[...]
    choice = head_choice(inner, head_size)
    before = through[0:1, :]
    state_ref[0] = (
        enter_ref[0] + head_column(before, head_choice_t(inner, head_size)) * coming
    ).astype(bf16)
    across = nt(q_ref[...], coming.astype(bf16))
    ssm = ssm_ref[...] + across * dot_pair(carry_factor(pos, decay) * before, choice)
    full_ref[...] = ssm
    through[...] = through[...] * passing_row(pos, decay)
    gate = gate_ref[...]
    gated = ssm * (gate * jax.nn.sigmoid(gate))
    gno = gno_ref[...]
    gain = gain_ref[...] * (pos[:, :1] >= 0.0).astype(f32)
    branch_ref[...] = nt((gated * gain).astype(bf16), out_ref[...]).astype(bf16)
    grad_unit = gno * gain
    squares = jnp.sum(gated * gated, axis=1, keepdims=True)
    dots = jnp.sum(grad_unit * gated, axis=1, keepdims=True)
    lanes = iota((STRETCH, LANES), 1)
    stats_ref[...] = jnp.where(lanes == 0, squares, dots).T[0:2]


def gate_back_kernel(
    dims, groups,
    pos_ref, stats_ref, ssm_ref, gate_ref, gno_ref, vkq_ref, decay_ref, gain_ref, skip_ref,
    gssm_ref, ggate_ref, low_ref, glog_ref, leave_ref, last_ref, sums_ref,
    back, through,
):
    heads, head_size, inner, states = dims
    step = pl.program_id(0)

    @pl.when(step == 0)
    def _():
        back[...] = jnp.zeros_like(back)
        through[...] = jnp.ones_like(through)
        sums_ref[...] = jnp.zeros_like(sums_ref)

    pos = column(pos_ref[0].astype(f32))
    valid = (pos[:, :1] >= 0.0).astype(f32)
    stats = column(stats_ref[...])
    scale = lax.rsqrt(stats[:, 0:1] / INNER + epsilon)
    dots = stats[:, 1:2]
    gate = gate_ref[...]
    ssm = ssm_ref[...]
    sig = jax.nn.sigmoid(gate)
    act = gate * sig
    gated = ssm * act
    unit = gated * scale
    gain = gain_ref[...]
    gno = gno_ref[...]
    low_ref[...] = (unit * gain * valid).astype(bf16)
    grad_unit = gno * gain * valid
    grad_gated = scale * (grad_unit - gated * (scale * scale * dots * (1.0 / INNER)))
    gssm = (grad_gated * act).astype(bf16)
    gssm_ref[...] = gssm
    ggate_ref[...] = (grad_gated * ssm * sig * (1.0 + gate * (1.0 - sig))).astype(bf16)
    g = gssm.astype(f32)
    value_f = vkq_ref[:, :inner].astype(f32)
    queries = vkq_ref[:, inner + states :]
    g_values = g * value_f
    choice = head_choice(inner, head_size)
    choice_t = head_choice_t(inner, head_size)
    glog_ref[...] = dot_pair(g * ssm - skip_ref[...] * g_values, choice_t)
    sums_ref[0:1, :] += jnp.sum(gno * unit * valid, axis=0, keepdims=True)
    sums_ref[1:2, :] += jnp.sum(g_values, axis=0, keepdims=True)
    decay = decay_ref[...]
    core = (g * dot_pair(carry_factor(pos, decay), choice)).astype(bf16)
    after = back[...]
    leave_ref[0] = after
    passing = passing_row(pos, decay)
    through[...] = through[...] * passing
    back[...] = tn(core, queries) + head_column(passing, choice_t) * after

    @pl.when(step == pl.num_programs(0) - 1)
    def _():
        pack_state(last_ref, back[...], through[0:1, :], heads // groups)


def scan_back_kernel(
    dims, first, blocks, groups, hops,
    pos_ref, tok_ref, w_ref, gain_ref, taps_ref, rate_ref, skip_ref, mixed_ref, before_ref,
    edge_ref, vkq_ref, gssm_ref, ggate_ref, glog_ref, step_ref, decay_ref, state_ref, leave_ref,
    gp_in, pp_in, suffix_in, gsum_in, tsum_in, hsum_in, *refs,
):
    go_refs, refs = refs[:hops], refs[hops:]
    part_ref, ret_ref, grads_ref, gp_out, pp_out, suffix, gsum_ref, tsum_ref, hsum_ref = refs[-14:-5]
    mx, gp, pp, edge, go = refs[-5:]
    heads, head_size, inner, states = dims
    width = inner + 2 * states
    at_mixed, at_misc = inner, inner + width
    step = pl.program_id(0)
    c = blocks - 1 - first - step

    @pl.when(step == 0)
    def _():
        for out, given in (
            (suffix, suffix_in), (gsum_ref, gsum_in), (tsum_ref, tsum_in), (hsum_ref, hsum_in)
        ):
            out[...] = given[...]
        go[...] = join_states(go_refs, head_choice_t(inner, head_size), groups)
        gp[STRETCH : STRETCH + 8, :] = gp_in[...]
        pp[STRETCH : STRETCH + 8, :] = pp_in[...]

    @pl.when(step > 0)
    def _():
        gp[STRETCH : STRETCH + 8, :] = gp[0:8, :]
        pp[STRETCH : STRETCH + 8, :] = pp[0:8, :]

    @pl.when(c == 0)
    def _():
        mx[0:8, :] = edge_ref[HALO - 8 :, :].astype(f32)

    @pl.when(c > 0)
    def _():
        mx[0:8, :] = before_ref[HALO - 8 :, :].astype(f32)

    pos = column(pos_ref[0].astype(f32))
    pp[0:STRETCH, :] = pos
    mx[8 : 8 + STRETCH, :] = mixed_ref[...].astype(f32)
    values = vkq_ref[:, :inner]
    keys = vkq_ref[:, inner : inner + states]
    queries = vkq_ref[:, inner + states :]
    value_f = values.astype(f32)
    gssm = gssm_ref[...]
    g = gssm.astype(f32)
    step_pre = step_ref[...]
    decay = decay_ref[...]
    decay_t = decay.T
    dt = steps_of(step_pre, pos, heads)
    rate = -jnp.exp(rate_ref[...])
    choice = head_choice(inner, head_size)
    choice_t = head_choice_t(inner, head_size)
    dt_wide = dot_pair(dt, choice)
    dt_values = (value_f * dt_wide).astype(bf16)
    mask = mask_matrix(pos)
    gram = nt(queries, keys)
    per = LANES // head_size
    grad_gram = None
    turned = []
    for pair in range(inner // LANES):
        lanes = slice(pair * LANES, (pair + 1) * LANES)
        total = None
        for k in range(per):
            h = pair * per + k
            spread = jnp.exp((decay[:, h : h + 1] - decay_t[h : h + 1, :]) + mask)
            own_g = pair_sel(gssm[:, lanes], k, head_size)
            term = tn((gram * spread).astype(bf16), own_g)
            total = term if total is None else total + term
            more = nt(own_g, dt_values[:, lanes]) * spread
            grad_gram = more if grad_gram is None else grad_gram + more
        turned.append(total)
    turned = jnp.concatenate(turned, axis=1)
    grad_gram = grad_gram.astype(bf16)
    entering = state_ref[0]
    after = suffix[0:1, :]
    leaving = leave_ref[0] + head_column(after, choice_t) * go[...]
    leaving_low = leaving.astype(bf16)
    passing = passing_row(pos, decay)
    suffix[...] = suffix[...] * passing
    far = end_factor(pos, decay)
    wend = far * dt
    wend_wide = dot_pair(wend, choice)
    keyed = nt(keys, leaving_low)
    core = (g * dot_pair(carry_factor(pos, decay), choice)).astype(bf16)
    grad_values = skip_ref[...] * g + dt_wide * turned + wend_wide * keyed
    grad_keys = tn(grad_gram, queries) + nn((value_f * wend_wide).astype(bf16), leaving_low)
    grad_queries = nn(grad_gram, keys) + nn(core, entering)
    within_dt = dot_pair(value_f * turned, choice_t)
    within_logs = dot_pair(dt_values.astype(f32) * turned, choice_t)
    grad_wend = dot_pair(value_f * keyed, choice_t)
    through = jnp.sum(leaving * entering.astype(f32), axis=1, keepdims=True)
    last_grad = passing * jnp.sum(through * choice_t.astype(f32), axis=0, keepdims=True)
    end_terms = grad_wend * wend
    grad_logs = glog_ref[...] - within_logs - end_terms
    at_last = iota((STRETCH, LANES), 0) == STRETCH - 1
    grad_logs = grad_logs + jnp.where(
        at_last, jnp.sum(end_terms, axis=0, keepdims=True) + last_grad, 0.0
    )
    tri = (iota((STRETCH, STRETCH), 1) >= iota((STRETCH, STRETCH), 0)).astype(bf16)
    grad_steps = dot_triple(tri, grad_logs)
    grad_dt = within_dt + grad_wend * far + grad_steps * rate
    lane_ok = (iota((STRETCH, LANES), 1) < heads) & (pos >= 0.0)
    grad_step = jnp.where(lane_ok, grad_dt * jax.nn.sigmoid(step_pre), 0.0)
    hsum_ref[0:1, :] += jnp.sum(grad_step, axis=0, keepdims=True)
    hsum_ref[1:2, :] += jnp.sum(grad_steps * dt, axis=0, keepdims=True) * rate

    conv = conv_of(mx, taps_ref, pos)
    sig = jax.nn.sigmoid(conv)
    grad_conv = jnp.concatenate([grad_values, grad_keys, grad_queries], axis=1)
    grad_pre = grad_conv * (sig * (1.0 + conv * (1.0 - sig)))
    gp[0:STRETCH, :] = grad_pre
    tsum_ref[CONV : CONV + 1, :] += jnp.sum(grad_pre, axis=0, keepdims=True)
    tsum_ref[CONV - 1 : CONV, :] += jnp.sum(
        grad_pre * mx[8 : 8 + STRETCH, :], axis=0, keepdims=True
    )
    grad_mixed = grad_pre * taps_ref[CONV - 1 : CONV, :]
    for s in range(1, CONV):
        inside = (pos[:, :1] >= float(s)).astype(f32)
        tsum_ref[CONV - 1 - s : CONV - s, :] += jnp.sum(
            grad_pre * inside * mx[8 - s : 8 - s + STRETCH, :], axis=0, keepdims=True
        )
        later = (pp[s : s + STRETCH, :][:, :1] >= float(s)).astype(f32)
        grad_mixed = grad_mixed + gp[s : s + STRETCH, :] * later * taps_ref[
            CONV - 1 - s : CONV - s, :
        ]
    grads = jnp.concatenate(
        [ggate_ref[...], grad_mixed.astype(bf16), grad_step.astype(bf16)], axis=1
    )
    partial = nt(grads, w_ref[...])
    unit = row_norm(tok_ref[...].astype(f32))[1]
    grads_ref[...] = grads[:, at_mixed:]
    gp_out[...] = gp[0:8, :]
    pp_out[...] = pp[0:8, :]
    part_ref[...] = partial.astype(bf16)
    gsum_ref[0:1, :] += jnp.sum(partial * unit, axis=0, keepdims=True)
    ret_ref[...] = jnp.zeros_like(ret_ref)

    @pl.when(c == 0)
    def _():
        edge[0:8, :] = jnp.zeros((8, width), f32)
        total = jnp.zeros((8, width), f32)
        for s in range(1, CONV):
            inside = (pos[0:8, :1] >= float(s)).astype(f32)
            edge[8:16, :] = gp[0:8, :] * inside
            total = total + edge[s : s + 8, :] * taps_ref[CONV - 1 - s : CONV - s, :]
        ret_ref[...] = total


def spread_rows(out_ref, total_ref, groups, cores):
    size = total_ref.shape[0] // (cores * groups)
    for at in range(cores * groups):
        out_ref[at % cores, at // cores] = total_ref[at * size : (at + 1) * size, :].astype(bf16)


def first_grad_kernel(
    dims, groups, cores, tok_ref, gain_ref, gate_ref, og_ref, low_ref, out_ref, total
):
    inner = dims[2]
    c = pl.program_id(0)

    @pl.when(c == 0)
    def _():
        total[...] = jnp.zeros_like(total)

    normed = (row_norm(tok_ref[...].astype(f32))[1] * gain_ref[0:1, :]).astype(bf16)
    total[:, :inner] += tn(normed, gate_ref[...])
    total[:, inner:] += tn(og_ref[...], low_ref[...])

    @pl.when(c == pl.num_programs(0) - 1)
    def _():
        spread_rows(out_ref, total, groups, cores)


def weight_grad_kernel(
    dims, groups, cores,
    tok_ref, gain_ref, grads_ref, extra_ref, gsum_ref, tail_ref,
    out_ref,
    total,
):
    heads, head_size, inner, states = dims
    width = inner + 2 * states
    c = pl.program_id(0)

    @pl.when(c == 0)
    def _():
        total[...] = jnp.zeros_like(total)

    unit = row_norm(tok_ref[...].astype(f32))[1]
    normed = (unit * gain_ref[0:1, :]).astype(bf16)
    total[...] += tn(normed, grads_ref[...])

    @pl.when(c == pl.num_programs(0) - 1)
    def _():
        total[:, :width] += tn(normed[STRETCH - HALO :], extra_ref[...])
        norm = gsum_ref[0:1, :] + jnp.sum(
            tail_ref[...] * unit[STRETCH - HALO :], axis=0, keepdims=True
        )
        norm = jnp.broadcast_to(norm, (LANES, norm.shape[1])).T
        misc = total[:, width:]
        total[:, width:] = jnp.where(iota(misc.shape, 1) == heads, norm, misc)
        spread_rows(out_ref, total, groups, cores)


def mixed_out_kernel(stats_ref, branch_ref, tok_ref, out_ref):
    scale = lax.rsqrt(column(stats_ref[...])[:, 0:1] / INNER + epsilon)
    out_ref[...] = (tok_ref[...].astype(f32) + scale * branch_ref[...].astype(f32)).astype(bf16)


def tokens_grad_kernel(grad_ref, tok_ref, og_ref, gain_ref, out_ref):
    scaling, unit = row_norm(tok_ref[...].astype(f32))
    grad = grad_ref[...].astype(f32) * gain_ref[0:1, :]
    mean = jnp.mean(grad * unit, axis=-1, keepdims=True)
    out_ref[...] = scaling * (grad - unit * mean) + og_ref[...].astype(f32)


def own_rows_kernel(mine_ref, came_ref, tok_ref, gain_ref, tail_ref, out_ref):
    scaling, unit = row_norm(tok_ref[...].astype(f32))
    grad = mine_ref[...].astype(f32) + came_ref[...].astype(f32)
    size, model = grad.shape
    tail = jnp.concatenate([jnp.zeros((size - HALO, model), f32), tail_ref[...]], axis=0)
    grad = grad + jnp.where(pl.program_id(0) == pl.num_programs(0) - 1, tail, 0.0)
    grad = grad * gain_ref[0:1, :]
    mean = jnp.mean(grad * unit, axis=-1, keepdims=True)
    out_ref[...] = (scaling * (grad - unit * mean)).astype(bf16)


def copy_kernel(in_ref, out_ref):
    out_ref[...] = in_ref[...]


def add_kernel(a_ref, b_ref, out_ref):
    out_ref[...] = a_ref[...].astype(f32) + b_ref[...].astype(f32)


def own_branch_kernel(stats_ref, mine_ref, came_ref, tok_ref, out_ref):
    scale = lax.rsqrt(column(stats_ref[...])[:, 0:1] / INNER + epsilon)
    branch = mine_ref[...].astype(f32) + came_ref[...].astype(f32)
    out_ref[...] = (tok_ref[...].astype(f32) + scale * branch).astype(bf16)


def per_device(
    tokens,
    norm_gain,
    inner_weight,
    state_weight,
    step_weight,
    inner_taps,
    state_taps,
    step_bias,
    log_rate,
    skip_gain,
    gated_gain,
    out_weight,
    out_grad,
    positions,
):
    shares = row_shares()
    share = lax.axis_index("tp") // (lax.axis_size("tp") // shares)
    all_rows, model = tokens.shape
    rows = all_rows // shares
    own_heads = step_bias.shape[0]
    own_inner = gated_gain.shape[0]
    head_size = own_inner // own_heads
    heads, inner = own_heads * shares, own_inner * shares
    states = state_weight.shape[1] // 2
    blocks = rows // STRETCH
    width = inner + 2 * states
    at_mixed, at_misc = inner, inner + width
    columns = at_misc + LANES
    dims = (heads, head_size, inner, states)
    parts = lax.axis_size("ctx") * shares

    def own_share(x, size):
        return x if shares == 1 else lax.dynamic_slice_in_dim(x, share * size, size)

    def joined(groups, begin, size):
        return [g[:, begin : begin + size] for g in groups]

    def steps_at(lane):
        return jnp.pad(step_weight, ((0, 0), (lane, LANES - lane - own_heads)))

    own_rows_of = norm_gain.shape[0]
    gain_lanes = jnp.concatenate(
        [
            jnp.zeros((own_rows_of, heads), bf16),
            norm_gain[:, None],
            jnp.zeros((own_rows_of, LANES - heads - 1), bf16),
        ],
        axis=1,
    )
    edge_rows = lax.ppermute(tokens[all_rows - HALO :], "ctx", [(0, 1)])
    all_tokens, all_grad = tokens, out_grad
    tokens, out_grad = own_share(tokens, rows), own_share(out_grad, rows)
    positions = own_share(positions, rows)
    halo_tokens = edge_rows
    if shares > 1:
        halo_tokens = jnp.where(share == 0, edge_rows, all_tokens[rows - HALO : rows])

    head_params = jnp.stack([step_bias, log_rate, skip_gain])
    small_own = jnp.concatenate(
        [
            jnp.pad(jnp.concatenate([inner_taps, gated_gain[None]]), ((0, 8 - CONV - 2), (0, 0))),
            jnp.pad(head_params, ((0, 5), (0, LANES - own_heads))),
        ],
        axis=1,
    )
    channels_in = [inner_weight[0], inner_weight[1]]
    near = gather_near(
        jnp.concatenate(channels_in + [state_weight, steps_at(0) + gain_lanes], axis=1)
    )
    stacks = gather_stacks(near)
    count = len(stacks)
    out_near = out_weight.T
    if shares > 1:
        more = swap_tp(jnp.concatenate(channels_in + [steps_at(own_heads)], axis=1), 2)
        near = gather_near(tied(more, tokens, out_grad, halo_tokens))
        out_more = swap_tp(tied(out_near, more), 2)
        small_more = swap_tp(tied(small_own, more), 2)
        near[-1] = tied(near[-1], out_more, small_more)
        stacks += gather_stacks(near)
        out_near = jnp.concatenate([out_near, out_more], axis=1)
    out_near = gather_near(tied(out_near, near[-1]))
    place = gather_place(own_rows_of)

    small_groups = [small_own] + ([small_more] if shares > 1 else [])
    channel_rows = jnp.concatenate(joined(small_groups, 0, own_inner), axis=1)
    head_rows = jnp.concatenate(joined(small_groups, own_inner, own_heads), axis=1)
    taps = jnp.concatenate(
        [channel_rows, jnp.pad(state_taps, ((0, 8 - CONV - 1), (0, 0)))], axis=1
    )
    gain_row = channel_rows[CONV + 1 : CONV + 2]
    skip_row = jnp.repeat(head_rows[2], head_size)[None, :]
    head_rows = jnp.pad(head_rows, ((0, 0), (0, LANES - heads)))
    bias_row, rate_row = head_rows[0:1], head_rows[1:2]
    pos_rows = positions.reshape(blocks, 1, STRETCH)

    def fixed(shape):
        return pl.BlockSpec(shape, lambda c: (0,) * len(shape))

    def by_rows(cols, order, at=0):
        return pl.BlockSpec((STRETCH, cols), lambda c: (order(c), at))

    def by_block(order):
        return pl.BlockSpec((1, inner, states), lambda c: (order(c), 0, 0))

    def pos_spec(order):
        return pl.BlockSpec((1, 1, STRETCH), lambda c: (order(c), 0, 0))

    def ahead(c):
        return c

    def reverse(c):
        return blocks - 1 - c

    def shape(*dims_of, dtype=f32):
        return jax.ShapeDtypeStruct(dims_of, dtype)

    light = pl.CostEstimate(flops=1024, bytes_accessed=1024, transcendentals=0)
    params = pltpu.CompilerParams(
        dimension_semantics=("arbitrary",), vmem_limit_bytes=VMEM_BYTES
    )

    scalars = pl.BlockSpec(memory_space=pltpu.SMEM)
    mixed, vkq, ssm_local, step_pre, decay, enter, last_state, edge, model_gain, weight = (
        pl.pallas_call(
            functools.partial(forward_kernel, dims, count, shares),
            grid=(blocks,),
            in_specs=[
                scalars,
                *[fixed(a.shape) for a in stacks],
                pos_spec(ahead),
                by_rows(model, ahead),
                fixed((HALO, model)),
                fixed((8, width)),
                fixed((1, LANES)),
                fixed((1, LANES)),
                fixed((1, inner)),
            ],
            out_specs=[
                by_rows(width, ahead),
                by_rows(width, ahead),
                by_rows(inner, ahead),
                by_rows(LANES, ahead),
                by_rows(LANES, ahead),
                by_block(ahead),
                fixed((inner + HALO, states)),
                fixed((HALO, width)),
                fixed((8, model)),
                fixed((model, columns)),
            ],
            out_shape=[
                shape(rows, width, dtype=bf16),
                shape(rows, width, dtype=bf16),
                shape(rows, inner),
                shape(rows, LANES),
                shape(rows, LANES),
                shape(blocks, inner, states),
                shape(inner + HALO, states, dtype=bf16),
                shape(HALO, width, dtype=bf16),
                shape(8, model),
                shape(model, columns, dtype=bf16),
            ],
            scratch_shapes=[
                pltpu.VMEM((STRETCH + 8, width), f32),
                pltpu.VMEM((inner, states), f32),
                pltpu.VMEM((8, LANES), f32),
            ],
            compiler_params=params,
            name="forward",
        )(
            place, *stacks, pos_rows, tokens, halo_tokens, taps, bias_row, rate_row, skip_row
        )
    )
    out_stacks = gather_stacks(out_near[:-1] + [tied(out_near[-1], last_state)])
    coming = [shift_part(last_state, by) for by in range(1, parts)]
    gate, grad_out, out_t = pl.pallas_call(
        functools.partial(gates_kernel, count),
        grid=(blocks,),
        in_specs=[
            scalars,
            *[fixed(a.shape) for a in out_stacks],
            by_rows(model, ahead),
            fixed((8, model)),
            pl.BlockSpec((model, inner), lambda c: (0, 0)),
            by_rows(model, ahead),
        ],
        out_specs=[by_rows(inner, ahead), by_rows(inner, ahead), fixed((model, inner))],
        out_shape=[shape(rows, inner), shape(rows, inner), shape(model, inner, dtype=bf16)],
        compiler_params=params,
        name="gates",
    )(place, *out_stacks, tokens, model_gain, weight, out_grad)
    ssm, state, stats, branch = pl.pallas_call(
        functools.partial(stats_kernel, dims, shares, parts - 1),
        grid=(blocks,),
        in_specs=[
            *[fixed((inner + HALO, states))] * (parts - 1),
            pos_spec(ahead),
            by_rows(inner, ahead),
            by_rows(inner, ahead),
            by_rows(states, ahead, (inner + states) // states),
            by_rows(LANES, ahead),
            by_block(ahead),
            by_rows(inner, ahead),
            fixed((model, inner)),
            fixed((1, inner)),
        ],
        out_specs=[
            by_rows(inner, ahead),
            by_block(ahead),
            pl.BlockSpec((2, STRETCH), lambda c: (0, c)),
            by_rows(model, ahead),
        ],
        out_shape=[
            shape(rows, inner),
            shape(blocks, inner, states, dtype=bf16),
            shape(2, rows),
            shape(rows, model, dtype=bf16),
        ],
        scratch_shapes=[pltpu.VMEM((8, LANES), f32), pltpu.VMEM((inner, states), f32)],
        compiler_params=params,
        name="stats",
    )(*coming, pos_rows, ssm_local, gate, vkq, decay, enter, grad_out, out_t, gain_row)
    half = rows // 2
    member = lax.axis_index("tp") % 2

    def halves(x):
        sent = lax.dynamic_slice_in_dim(x, (1 - member) * half, half)
        return lax.dynamic_slice_in_dim(tied(x, sent), member * half, half), swap_tp(sent, 1)

    if shares > 1:
        own_tokens = lax.dynamic_slice_in_dim(tokens, member * half, half)
        stats = stats + swap_tp(stats, 1)
        own_branch = pl.pallas_call(
            own_branch_kernel,
            grid=(half // STRETCH,),
            in_specs=[pl.BlockSpec((2, STRETCH), lambda c: (0, c))]
            + [by_rows(model, ahead)] * 3,
            out_specs=by_rows(model, ahead),
            out_shape=shape(half, model, dtype=bf16),
            compiler_params=params,
            name="own_branch",
        )(
            lax.dynamic_slice_in_dim(stats, member * half, half, 1),
            *halves(tied(branch, stats)),
            own_tokens,
        )
    else:
        stats = sum_tp_small(stats)
        first_total = lax.psum(branch, "tp")
    grad_ssm, grad_gate, normed_out, grad_logs, leave, last_back, gate_sums = pl.pallas_call(
        functools.partial(gate_back_kernel, dims, shares),
        grid=(blocks,),
        in_specs=[
            pos_spec(reverse),
            pl.BlockSpec((2, STRETCH), lambda c: (0, reverse(c))),
            by_rows(inner, reverse),
            by_rows(inner, reverse),
            by_rows(inner, reverse),
            by_rows(width, reverse),
            by_rows(LANES, reverse),
            fixed((1, inner)),
            fixed((1, inner)),
        ],
        out_specs=[
            by_rows(inner, reverse),
            by_rows(inner, reverse),
            by_rows(inner, reverse),
            by_rows(LANES, reverse),
            by_block(reverse),
            fixed((inner + HALO, states)),
            fixed((8, inner)),
        ],
        out_shape=[
            shape(rows, inner, dtype=bf16),
            shape(rows, inner, dtype=bf16),
            shape(rows, inner, dtype=bf16),
            shape(rows, LANES),
            shape(blocks, inner, states),
            shape(inner + HALO, states, dtype=bf16),
            shape(8, inner),
        ],
        scratch_shapes=[pltpu.VMEM((inner, states), f32), pltpu.VMEM((8, LANES), f32)],
        compiler_params=params,
        cost_estimate=light,
        name="gate_back",
    )(pos_rows, stats, ssm, gate, grad_out, vkq, decay, gain_row, skip_row)
    going = [shift_part(last_back, -by) for by in range(1, parts)]
    if shares > 1:
        first_gather = lax.all_gather(tied(own_branch, *going), "tp", axis=0, tiled=True)
        mixed_out = pl.pallas_call(
            copy_kernel,
            grid=(all_rows // STRETCH,),
            in_specs=[by_rows(model, ahead)],
            out_specs=by_rows(model, ahead),
            out_shape=shape(all_rows, model, dtype=bf16),
            compiler_params=params,
            name="mixed_out",
        )(first_gather)
        first_total = first_gather[:8, :LANES]
    near_count, cores = (lax.axis_size("fsdp"), lax.axis_size("ctx")) if small_mesh() else (1, 1)

    def grad_shape(cols):
        return (cores, near_count, model // (cores * near_count), cols)

    per_halo = STRETCH // HALO

    def scan_piece(first, size, going, carried):
        def place_of(c):
            return blocks - 1 - first - c

        grads_before, *carried = carried
        carry_shapes = [a.shape for a in carried]
        aliases = {}
        in_specs = [
            pos_spec(place_of),
            by_rows(model, place_of),
            fixed((model, columns)),
            fixed((8, model)),
            fixed((8, width)),
            fixed((1, LANES)),
            fixed((1, inner)),
            by_rows(width, place_of),
            pl.BlockSpec(
                (HALO, width), lambda c: (jnp.maximum(place_of(c) * per_halo - 1, 0), 0)
            ),
            fixed((HALO, width)),
            by_rows(width, place_of),
            by_rows(inner, place_of),
            by_rows(inner, place_of),
            by_rows(LANES, place_of),
            by_rows(LANES, place_of),
            by_rows(LANES, place_of),
            by_block(place_of),
            by_block(place_of),
            *[fixed(a) for a in carry_shapes],
            *[fixed((inner + HALO, states))] * (parts - 1),
        ]
        operands = [
            pos_rows, tokens, weight, model_gain, taps, rate_row, skip_row, mixed, mixed, edge,
            vkq, grad_ssm, grad_gate, grad_logs, step_pre, decay, state, leave, *carried, *going,
        ]
        if grads_before is not None:
            aliases = {len(operands): 2}
            operands.append(grads_before)
            in_specs.append(pl.BlockSpec(memory_space=pl.ANY))
        return pl.pallas_call(
            functools.partial(scan_back_kernel, dims, first, blocks, shares, parts - 1),
            grid=(size,),
            in_specs=in_specs,
            out_specs=[
                pl.BlockSpec((STRETCH, model), lambda c: (size - 1 - c, 0)),
                fixed((8, width)),
                by_rows(columns - inner, place_of),
                *[fixed(a) for a in carry_shapes],
            ],
            out_shape=[
                shape(size * STRETCH, model, dtype=bf16),
                shape(8, width),
                shape(rows, columns - inner, dtype=bf16),
                *[shape(*a) for a in carry_shapes],
            ],
            input_output_aliases=aliases,
            scratch_shapes=[
                pltpu.VMEM((STRETCH + 8, width), f32),
                pltpu.VMEM((STRETCH + 8, width), f32),
                pltpu.VMEM((STRETCH + 8, LANES), f32),
                pltpu.VMEM((16, width), f32),
                pltpu.VMEM((inner, states), f32),
            ],
            compiler_params=params,
            cost_estimate=light,
        name="scan_back",
        )(*operands)

    carried = [
        None,
        jnp.zeros((8, width), f32),
        jnp.zeros((8, LANES), f32),
        jnp.ones((8, LANES), f32),
        jnp.zeros((8, model), f32),
        jnp.zeros((8, width), f32),
        jnp.zeros((8, LANES), f32),
    ]
    partial, returned, *carried = scan_piece(0, blocks, going, carried)
    grads, _, _, _, norm_sums, tap_sums, head_sums = carried

    small = jnp.concatenate([tap_sums.reshape(-1, LANES), gate_sums.reshape(-1, LANES), head_sums])
    if shares > 1:
        mine, came = halves(partial)
        small = tied(small, mine)
        normed_out = tied(normed_out, mine)
    first_grad = pl.pallas_call(
        functools.partial(first_grad_kernel, dims, near_count, cores),
        grid=(blocks,),
        in_specs=[
            by_rows(model, ahead),
            fixed((8, model)),
            by_rows(inner, ahead),
            by_rows(model, ahead),
            by_rows(inner, ahead),
        ],
        out_specs=fixed(grad_shape(2 * inner)),
        out_shape=shape(*grad_shape(2 * inner), dtype=bf16),
        scratch_shapes=[pltpu.VMEM((model, 2 * inner), f32)],
        compiler_params=params,
        cost_estimate=light,
        name="first_grad",
    )(tokens, model_gain, grad_gate, out_grad, normed_out)
    small = sum_rows_group(small)
    extra = shift_part(returned, -1).astype(bf16)
    if shares > 1:
        extra = jnp.concatenate(
            [extra[:, own_inner:inner], extra[:, :own_inner], extra[:, inner:]], axis=1
        )
    extra = jnp.concatenate([jnp.zeros((HALO - 8, width), bf16), extra], axis=0)
    tail_part = nt(extra, weight[:, at_mixed:at_misc])

    if shares > 1:
        tail_low = tail_part.astype(bf16)
        tail_sum = tail_low.astype(f32) + swap_tp(tail_low, 1).astype(f32)
        tail_sum = jnp.where(member == 1, tail_sum, 0.0)
        own_rows = pl.pallas_call(
            own_rows_kernel,
            grid=(half // STRETCH,),
            in_specs=[by_rows(model, ahead)] * 3 + [fixed((8, model)), fixed((HALO, model))],
            out_specs=by_rows(model, ahead),
            out_shape=shape(half, model, dtype=bf16),
            compiler_params=params,
            name="own_rows",
        )(tied(mine, first_grad), came, own_tokens, model_gain, tail_sum)
        grads = tied(grads, own_rows, first_total)
        own_rows = tied(own_rows, first_total)
        second_total = lax.all_gather(own_rows, "tp", axis=0, tiled=True)
    else:
        partial = partial.at[rows - HALO :].add(tail_part.astype(bf16))
        partial = tied(partial, first_total)
        mixed_out = pl.pallas_call(
            mixed_out_kernel,
            grid=(blocks,),
            in_specs=[
                pl.BlockSpec((2, STRETCH), lambda c: (0, c)),
                by_rows(model, ahead),
                by_rows(model, ahead),
            ],
            out_specs=by_rows(model, ahead),
            out_shape=shape(rows, model, dtype=bf16),
            compiler_params=params,
            name="mixed_out",
        )(stats, first_total, tokens)
        tokens_grad = pl.pallas_call(
            tokens_grad_kernel,
            grid=(blocks,),
            in_specs=[by_rows(model, ahead)] * 3 + [fixed((8, model))],
            out_specs=by_rows(model, ahead),
            out_shape=shape(rows, model),
            compiler_params=params,
            name="tokens_grad",
        )(lax.psum(partial, "tp"), tokens, out_grad, model_gain)

    weight_grad = pl.pallas_call(
        functools.partial(weight_grad_kernel, dims, near_count, cores),
        grid=(blocks,),
        in_specs=[
            by_rows(model, ahead),
            fixed((8, model)),
            by_rows(columns - inner, ahead),
            fixed((HALO, width)),
            fixed((8, model)),
            fixed((HALO, model)),
        ],
        out_specs=fixed(grad_shape(columns - inner)),
        out_shape=shape(*grad_shape(columns - inner), dtype=bf16),
        scratch_shapes=[pltpu.VMEM((model, columns - inner), f32)],
        compiler_params=params,
        cost_estimate=light,
        name="weight_grad",
    )(tokens, model_gain, grads, extra, norm_sums, tail_part)
    first_grad = scatter_rows(first_grad)
    if shares > 1:
        second_total = tied(second_total, mixed_out[:8, :LANES])
        tokens_grad = pl.pallas_call(
            add_kernel,
            grid=(all_rows // STRETCH,),
            in_specs=[by_rows(model, ahead)] * 2,
            out_specs=by_rows(model, ahead),
            out_shape=shape(all_rows, model),
            compiler_params=params,
            name="tokens_grad",
        )(second_total, all_grad)
    late_grad = scatter_rows(weight_grad)
    at = 8 * width // LANES
    tap_total = small[:at].reshape(8, width)
    gate_total = small[at : at + 8 * inner // LANES].reshape(8, inner)
    head_total = small[at + 8 * inner // LANES :]
    shared = late_grad[:, inner:].astype(bf16)
    state_taps_grad = tap_total[: CONV + 1, inner:]
    rows_of = jnp.concatenate([tap_total[: CONV + 1, :inner], gate_total[:2]])
    channels_of = [first_grad[:, :inner], late_grad[:, :inner], first_grad[:, inner:]]
    steps_of_grad = late_grad[:, width:]
    groups = [g[:, :own_inner] for g in channels_of] + [steps_of_grad[:, :own_heads]]
    channel_total, head_total = rows_of[:, :own_inner], head_total[:2, :LANES]
    if shares > 1:
        sent = [g[:, own_inner:] for g in channels_of]
        sent.append(steps_of_grad[:, own_heads:])
        sent.append(jnp.zeros((steps_of_grad.shape[0], own_heads), f32))
        sent = jnp.concatenate(sent, axis=1).astype(bf16)
        few = jnp.concatenate(
            [
                jnp.pad(rows_of[:, own_inner:], ((0, 1), (0, 0))),
                jnp.pad(
                    head_total[:, own_heads : own_heads + LANES // 2], ((0, 6), (0, LANES // 2))
                ),
            ],
            axis=1,
        )
        pair = (shared.astype(f32) + swap_tp(shared, 1).astype(f32)).astype(bf16)
        taps_pair = state_taps_grad + swap_tp(state_taps_grad, 1)
        came, few = swap_tp(sent, 2).astype(f32), swap_tp(few, 2)
        groups = [
            g + came[:, k * own_inner : k * own_inner + g.shape[1]] for k, g in enumerate(groups)
        ]
        channel_total = channel_total + few[: CONV + 3, :own_inner]
        head_total = head_total[:, :own_heads] + few[:2, own_inner : own_inner + own_heads]
        pair_more = tied(swap_tp(pair, 2), tokens_grad[:8, :LANES])
        shared = pair.astype(f32) + pair_more.astype(f32)
        state_taps_grad = taps_pair + swap_tp(taps_pair, 2)
    else:
        shared = sum_tp_small(shared)
        state_taps_grad = sum_tp_small(state_taps_grad)
        head_total = head_total[:, :own_heads]
    state_weight_grad = shared[:, : 2 * states]
    norm_gain_grad = shared[:, 2 * states + heads]
    inner_weight_grad = jnp.stack(groups[:2])
    out_weight_grad = groups[2].T
    return (
        mixed_out,
        tokens_grad,
        norm_gain_grad,
        inner_weight_grad,
        state_weight_grad,
        groups[3],
        channel_total[: CONV + 1],
        state_taps_grad,
        head_total[0],
        head_total[1],
        jnp.sum(channel_total[CONV + 2].reshape(own_heads, head_size), axis=1),
        channel_total[CONV + 1],
        out_weight_grad,
    )


def solution(mesh):
    return jax.shard_map(
        per_device,
        mesh=mesh,
        in_specs=(
            P(("fsdp", "ctx"), None),
            P(("fsdp", "ctx")),
            P(None, ("fsdp", "ctx"), "tp"),
            P(("fsdp", "ctx"), None),
            P(("fsdp", "ctx"), "tp"),
            P(None, "tp"),
            P(),
            P("tp"),
            P("tp"),
            P("tp"),
            P("tp"),
            P("tp", ("fsdp", "ctx")),
            P(("fsdp", "ctx"), None),
            P(("fsdp", "ctx")),
        ),
        out_specs=(
            P(("fsdp", "ctx"), None),
            P(("fsdp", "ctx"), None),
            P(("fsdp", "ctx")),
            P(None, ("fsdp", "ctx"), "tp"),
            P(("fsdp", "ctx"), None),
            P(("fsdp", "ctx"), "tp"),
            P(None, "tp"),
            P(),
            P("tp"),
            P("tp"),
            P("tp"),
            P("tp"),
            P("tp", ("fsdp", "ctx")),
        ),
        check_vma=False,
    )
```

```python
import functools

import jax
import jax.numpy as jnp
from jax import lax
from jax.experimental import pallas as pl
from jax.experimental.pallas import tpu as pltpu
from jax.sharding import PartitionSpec as P

CONV = 4
STRETCH = 256
INNER = 2048
LANES = 128
HALO = 16
NEVER = -1e30
VMEM_BYTES = 60 * 1024 * 1024

epsilon = 1e-05
bf16 = jnp.bfloat16
f32 = jnp.float32


def swap_ctx(x):
    return lax.ppermute(x, "ctx", [(0, 1), (1, 0)])


def swap_fsdp(x, k):
    return lax.ppermute(x, "fsdp", [(i, i ^ k) for i in range(4)])


def swap_tp(x, k):
    return lax.ppermute(x, "tp", [(i, i ^ k) for i in range(4)])


def row_shares():
    return 2 if small_mesh() and lax.axis_size("tp") == 4 else 1


def shift_part(x, by):
    tp, shares = lax.axis_size("tp"), row_shares()
    parts, group = lax.axis_size("ctx") * shares, tp // shares

    def device(part, k):
        return part // shares * tp + part % shares * group + k

    pairs = [
        (device(part, k), device(part + by, k))
        for part in range(parts)
        if 0 <= part + by < parts
        for k in range(group)
    ]
    return lax.ppermute(x, ("ctx", "tp"), pairs)


def small_mesh():
    return lax.axis_size("fsdp") == 4 and lax.axis_size("ctx") == 2


def gather_near(x):
    if not small_mesh():
        return [lax.all_gather(x, ("fsdp", "ctx"), axis=0, tiled=True)]
    return [x] + [swap_fsdp(x, k) for k in (1, 2, 3)]


def gather_stacks(near):
    stack = jnp.stack(near)
    return [stack, swap_ctx(stack)] if small_mesh() else [stack]


def gather_place(size):
    if not small_mesh():
        return jnp.zeros((1,), jnp.int32)
    me = lax.axis_index("fsdp")
    core = lax.axis_index("ctx")
    place = [(me ^ k) * 2 + core for k in range(4)] + [(me ^ k) * 2 + 1 - core for k in range(4)]
    return (jnp.stack(place) * size).astype(jnp.int32)


def scatter_rows(x):
    if not small_mesh():
        x = x.reshape(-1, x.shape[-1])
        return lax.psum_scatter(x, ("fsdp", "ctx"), scatter_dimension=0, tiled=True).astype(f32)
    me = lax.axis_index("fsdp")
    core = lax.axis_index("ctx")
    theirs = swap_ctx(lax.dynamic_index_in_dim(x, 1 - core, 0, False))
    mine = lax.dynamic_index_in_dim(x, core, 0, False)
    summed = (mine.astype(f32) + theirs.astype(f32)).astype(bf16)
    total = lax.dynamic_index_in_dim(summed, me, 0, False).astype(f32)
    for k in (1, 2, 3):
        total = total + swap_fsdp(lax.dynamic_index_in_dim(summed, me ^ k, 0, False), k).astype(f32)
    return total


def sum_rows_group(x):
    if not small_mesh():
        return lax.psum(x, ("fsdp", "ctx"))
    x = x + swap_ctx(x)
    x = x + swap_fsdp(x, 1)
    return x + swap_fsdp(x, 2)


def sum_tp_small(x):
    if lax.axis_size("tp") != 4:
        return lax.psum(x, "tp").astype(f32)
    pair = (x.astype(f32) + swap_tp(x, 1).astype(f32)).astype(x.dtype)
    return pair.astype(f32) + swap_tp(pair, 2).astype(f32)


def tied(x, *others):
    return lax.optimization_barrier((x,) + others)[0]


def nn(a, b):
    return jnp.dot(a, b, preferred_element_type=f32)


def nt(a, b):
    return lax.dot_general(a, b, (((1,), (1,)), ((), ())), preferred_element_type=f32)


def tn(a, b):
    return lax.dot_general(a, b, (((0,), (0,)), ((), ())), preferred_element_type=f32)


def two_terms(x):
    high = x.astype(bf16)
    return high, (x - high.astype(f32)).astype(bf16)


def dot_pair(x, choice):
    high, low = two_terms(x)
    return nn(high, choice) + nn(low, choice)


def dot_triple(choice, x):
    high = x.astype(bf16)
    rest = x - high.astype(f32)
    middle, low = two_terms(rest)
    return nn(choice, high) + nn(choice, middle) + nn(choice, low)


def iota(shape, axis):
    return lax.broadcasted_iota(jnp.int32, shape, axis)


def head_choice(channels, head_size):
    return (iota((LANES, channels), 1) // head_size == iota((LANES, channels), 0)).astype(bf16)


def head_choice_t(channels, head_size):
    return (iota((channels, LANES), 0) // head_size == iota((channels, LANES), 1)).astype(bf16)


def head_column(row, choice_t):
    return jnp.sum(choice_t.astype(f32) * row, axis=1, keepdims=True)


def column(rows):
    if rows.shape[0] == 1:
        return jnp.broadcast_to(rows, (LANES, STRETCH)).T
    return jnp.concatenate([rows, jnp.zeros((LANES - rows.shape[0], STRETCH), f32)], axis=0).T


def row_norm(rows):
    scaling = lax.rsqrt(jnp.mean(rows * rows, axis=-1, keepdims=True) + epsilon)
    return scaling, rows * scaling


def softplus(v):
    return jnp.maximum(v, 0.0) + jnp.log1p(jnp.exp(-jnp.abs(v)))


def pair_sel(x, part, head_size):
    return jnp.where(iota(x.shape, 1) // head_size == part, x, jnp.zeros_like(x))


def mask_matrix(pos):
    wide = jnp.concatenate([pos] * (STRETCH // LANES), axis=1)
    ahead = (iota((STRETCH, STRETCH), 0) - iota((STRETCH, STRETCH), 1)).astype(f32)
    return jnp.where((ahead >= 0.0) & (ahead <= wide), 0.0, NEVER)


def carry_factor(pos, decay):
    places = iota((STRETCH, LANES), 0).astype(f32)
    return jnp.where(pos >= places + 1.0, jnp.exp(decay), 0.0)


def passing_row(pos, decay):
    last = slice(STRETCH - 1, STRETCH)
    return jnp.where(pos[last] >= float(STRETCH), jnp.exp(decay[last]), 0.0)


def pack_state(ref, state, through, own_heads):
    channels = state.shape[0]
    ref[:channels, :] = state.astype(bf16)
    row, col = iota((LANES, LANES), 0), iota((LANES, LANES), 1)
    turn = (row < 2 * own_heads) & (
        jnp.where(row < own_heads, row + own_heads, row - own_heads) == col
    )
    low = jnp.broadcast_to(through, (8, LANES))
    turned = dot_pair(low, turn.astype(bf16))
    ref[channels:, :] = jnp.concatenate([low, turned], axis=0).astype(bf16)


def join_states(refs, choice_t, groups):
    channels = choice_t.shape[0]
    half = channels // 2
    total = None
    for distance in range(len(refs), 0, -1):
        ref = refs[distance - 1]
        state = ref[:channels, :].astype(f32)
        through = ref[channels:, :].astype(f32)
        if groups == 2 and distance % 2 == 1:
            state = jnp.concatenate([state[half:], state[:half]], axis=0)
            through = through[8:9]
        else:
            through = through[0:1]
        total = state if total is None else state + head_column(through, choice_t) * total
    return total


def end_factor(pos, decay):
    last = slice(STRETCH - 1, STRETCH)
    places = iota((STRETCH, LANES), 0).astype(f32)
    return jnp.where(places >= STRETCH - 1.0 - pos[last], jnp.exp(decay[last] - decay), 0.0)


def steps_of(step_pre, pos, heads):
    lanes = iota((STRETCH, LANES), 1)
    return jnp.where((lanes < heads) & (pos >= 0.0), softplus(step_pre), 0.0)


def conv_of(mx_ref, taps_ref, pos):
    total = taps_ref[CONV : CONV + 1, :] + taps_ref[CONV - 1 : CONV, :] * mx_ref[8 : 8 + STRETCH, :]
    for s in range(1, CONV):
        window = mx_ref[8 - s : 8 - s + STRETCH, :] * (pos[:, :1] >= float(s)).astype(f32)
        total = total + taps_ref[CONV - 1 - s : CONV - s, :] * window
    return total


def place_stacks(place_ref, stacks, write):
    number = 0
    for stack in stacks:
        size = stack.shape[1]
        for k in range(stack.shape[0]):
            write(pl.ds(pl.multiple_of(place_ref[number], size), size), stack[k])
            number += 1


def forward_kernel(dims, count, groups, place_ref, *refs):
    own_stacks, refs = refs[:count], refs[count:]
    more_stacks, refs = refs[: count * (groups - 1)], refs[count * (groups - 1) :]
    pos_ref, tok_ref, halo_ref, taps_ref, bias_ref, rate_ref, skip_ref = refs[:7]
    mixed_ref, vkq_ref, ssm_ref, step_ref, decay_ref, enter_ref, last_ref = refs[7:14]
    edge_ref, gain_ref, w_ref, mx, state, through = refs[14:]
    heads, head_size, inner, states = dims
    width = inner + 2 * states
    at_mixed, at_misc = inner, inner + width
    c = pl.program_id(0)

    @pl.when(c == 0)
    def _():
        own = inner // groups

        def write_own(at, piece):
            w_ref[at, 0:own] = piece[:, 0:own]
            w_ref[at, at_mixed : at_mixed + own] = piece[:, own : 2 * own]
            w_ref[at, at_mixed + inner : at_misc] = piece[:, 2 * own : 2 * own + 2 * states]
            w_ref[at, at_misc:] = piece[:, 2 * own + 2 * states :]

        def write_more(at, piece):
            w_ref[at, own:inner] = piece[:, 0:own]
            w_ref[at, at_mixed + own : at_mixed + inner] = piece[:, own : 2 * own]
            w_ref[at, at_misc:] = w_ref[at, at_misc:] + piece[:, 2 * own :]

        place_stacks(place_ref, own_stacks, write_own)
        place_stacks(place_ref, more_stacks, write_more)
        misc = w_ref[:, at_misc:].astype(f32).T
        gain_ref[...] = jnp.broadcast_to(misc[heads : heads + 1], gain_ref.shape)
        unit = row_norm(halo_ref[...].astype(f32))[1]
        low = (unit * gain_ref[0:1, :]).astype(bf16)
        edge = nn(low, w_ref[:, at_mixed:at_misc]).astype(bf16)
        edge_ref[...] = edge
        mx[0:8, :] = edge[HALO - 8 :].astype(f32)
        state[...] = jnp.zeros_like(state)
        through[...] = jnp.ones_like(through)

    @pl.when(c > 0)
    def _():
        mx[0:8, :] = mx[STRETCH : STRETCH + 8, :]

    pos = column(pos_ref[0].astype(f32))
    unit = row_norm(tok_ref[...].astype(f32))[1]
    normed = (unit * gain_ref[0:1, :]).astype(bf16)
    mixed = nn(normed, w_ref[:, at_mixed:at_misc]).astype(bf16)
    mixed_ref[...] = mixed
    mx[8 : 8 + STRETCH, :] = mixed.astype(f32)
    step_pre = nn(normed, w_ref[:, at_misc:]) + bias_ref[...]
    step_ref[...] = step_pre
    conv = conv_of(mx, taps_ref, pos)
    vkq = (conv * jax.nn.sigmoid(conv)).astype(bf16)
    vkq_ref[...] = vkq
    values, keys, queries = vkq[:, :inner], vkq[:, inner : inner + states], vkq[:, inner + states :]
    dt = steps_of(step_pre, pos, heads)
    rate = -jnp.exp(rate_ref[...])
    tri = (iota((STRETCH, STRETCH), 1) <= iota((STRETCH, STRETCH), 0)).astype(bf16)
    decay = dot_triple(tri, dt * rate)
    decay_ref[...] = decay
    decay_t = decay.T
    mask = mask_matrix(pos)
    gram = nt(queries, keys)
    choice = head_choice(inner, head_size)
    value_f = values.astype(f32)
    dt_values = (value_f * dot_pair(dt, choice)).astype(bf16)
    per = LANES // head_size
    within = []
    for pair in range(inner // LANES):
        part = dt_values[:, pair * LANES : (pair + 1) * LANES]
        total = None
        for k in range(per):
            h = pair * per + k
            m = (gram * jnp.exp((decay[:, h : h + 1] - decay_t[h : h + 1, :]) + mask)).astype(bf16)
            term = nn(m, pair_sel(part, k, head_size))
            total = term if total is None else total + term
        within.append(total)
    within = jnp.concatenate(within, axis=1)
    entering = state[...]
    enter_ref[0] = entering
    across = nt(queries, entering.astype(bf16)) * dot_pair(carry_factor(pos, decay), choice)
    ssm_ref[...] = within + across + skip_ref[...] * value_f
    wend = end_factor(pos, decay) * dt
    fresh = tn((value_f * dot_pair(wend, choice)).astype(bf16), keys)
    passing = passing_row(pos, decay)
    through[...] = through[...] * passing
    state[...] = head_column(passing, head_choice_t(inner, head_size)) * entering + fresh

    @pl.when(c == pl.num_programs(0) - 1)
    def _():
        pack_state(last_ref, state[...], through[0:1, :], heads // groups)


def gates_kernel(count, place_ref, *refs):
    stacks, refs = refs[:count], refs[count:]
    tok_ref, gain_ref, w_ref, og_ref, gate_ref, gno_ref, out_ref = refs

    @pl.when(pl.program_id(0) == 0)
    def _():
        def write(at, piece):
            out_ref[at, :] = piece

        place_stacks(place_ref, stacks, write)

    normed = (row_norm(tok_ref[...].astype(f32))[1] * gain_ref[0:1, :]).astype(bf16)
    gate_ref[...] = nn(normed, w_ref[...])
    gno_ref[...] = nn(og_ref[...], out_ref[...])


def stats_kernel(dims, groups, hops, *refs):
    come_refs, refs = refs[:hops], refs[hops:]
    pos_ref, ssm_ref, gate_ref, q_ref, decay_ref, enter_ref, gno_ref, out_ref, gain_ref = refs[:9]
    full_ref, state_ref, stats_ref, branch_ref, through, come = refs[9:]
    heads, head_size, inner, states = dims
    c = pl.program_id(0)

    @pl.when(c == 0)
    def _():
        through[...] = jnp.ones_like(through)
        come[...] = join_states(come_refs, head_choice_t(inner, head_size), groups)

    pos = column(pos_ref[0].astype(f32))
    decay = decay_ref[...]
    coming = come[...]
    choice = head_choice(inner, head_size)
    before = through[0:1, :]
    state_ref[0] = (
        enter_ref[0] + head_column(before, head_choice_t(inner, head_size)) * coming
    ).astype(bf16)
    across = nt(q_ref[...], coming.astype(bf16))
    ssm = ssm_ref[...] + across * dot_pair(carry_factor(pos, decay) * before, choice)
    full_ref[...] = ssm
    through[...] = through[...] * passing_row(pos, decay)
    gate = gate_ref[...]
    gated = ssm * (gate * jax.nn.sigmoid(gate))
    gno = gno_ref[...]
    gain = gain_ref[...] * (pos[:, :1] >= 0.0).astype(f32)
    branch_ref[...] = nt((gated * gain).astype(bf16), out_ref[...]).astype(bf16)
    grad_unit = gno * gain
    squares = jnp.sum(gated * gated, axis=1, keepdims=True)
    dots = jnp.sum(grad_unit * gated, axis=1, keepdims=True)
    lanes = iota((STRETCH, LANES), 1)
    stats_ref[...] = jnp.where(lanes == 0, squares, dots).T[0:2]


def gate_back_kernel(
    dims, groups,
    pos_ref, stats_ref, ssm_ref, gate_ref, gno_ref, vkq_ref, decay_ref, gain_ref, skip_ref,
    gssm_ref, ggate_ref, low_ref, glog_ref, leave_ref, last_ref, sums_ref,
    back, through,
):
    heads, head_size, inner, states = dims
    step = pl.program_id(0)

    @pl.when(step == 0)
    def _():
        back[...] = jnp.zeros_like(back)
        through[...] = jnp.ones_like(through)
        sums_ref[...] = jnp.zeros_like(sums_ref)

    pos = column(pos_ref[0].astype(f32))
    valid = (pos[:, :1] >= 0.0).astype(f32)
    stats = column(stats_ref[...])
    scale = lax.rsqrt(stats[:, 0:1] / INNER + epsilon)
    dots = stats[:, 1:2]
    gate = gate_ref[...]
    ssm = ssm_ref[...]
    sig = jax.nn.sigmoid(gate)
    act = gate * sig
    gated = ssm * act
    unit = gated * scale
    gain = gain_ref[...]
    gno = gno_ref[...]
    low_ref[...] = (unit * gain * valid).astype(bf16)
    grad_unit = gno * gain * valid
    grad_gated = scale * (grad_unit - gated * (scale * scale * dots * (1.0 / INNER)))
    gssm = (grad_gated * act).astype(bf16)
    gssm_ref[...] = gssm
    ggate_ref[...] = (grad_gated * ssm * sig * (1.0 + gate * (1.0 - sig))).astype(bf16)
    g = gssm.astype(f32)
    value_f = vkq_ref[:, :inner].astype(f32)
    queries = vkq_ref[:, inner + states :]
    g_values = g * value_f
    choice = head_choice(inner, head_size)
    choice_t = head_choice_t(inner, head_size)
    glog_ref[...] = dot_pair(g * ssm - skip_ref[...] * g_values, choice_t)
    sums_ref[0:1, :] += jnp.sum(gno * unit * valid, axis=0, keepdims=True)
    sums_ref[1:2, :] += jnp.sum(g_values, axis=0, keepdims=True)
    decay = decay_ref[...]
    core = (g * dot_pair(carry_factor(pos, decay), choice)).astype(bf16)
    after = back[...]
    leave_ref[0] = after
    passing = passing_row(pos, decay)
    through[...] = through[...] * passing
    back[...] = tn(core, queries) + head_column(passing, choice_t) * after

    @pl.when(step == pl.num_programs(0) - 1)
    def _():
        pack_state(last_ref, back[...], through[0:1, :], heads // groups)


def scan_back_kernel(
    dims, first, blocks, groups, hops,
    pos_ref, tok_ref, w_ref, gain_ref, taps_ref, rate_ref, skip_ref, mixed_ref, before_ref,
    edge_ref, vkq_ref, gssm_ref, ggate_ref, glog_ref, step_ref, decay_ref, state_ref, leave_ref,
    gp_in, pp_in, suffix_in, gsum_in, tsum_in, hsum_in, *refs,
):
    go_refs, refs = refs[:hops], refs[hops:]
    part_ref, ret_ref, grads_ref, gp_out, pp_out, suffix, gsum_ref, tsum_ref, hsum_ref = refs[-14:-5]
    mx, gp, pp, edge, go = refs[-5:]
    heads, head_size, inner, states = dims
    width = inner + 2 * states
    at_mixed, at_misc = inner, inner + width
    step = pl.program_id(0)
    c = blocks - 1 - first - step

    @pl.when(step == 0)
    def _():
        for out, given in (
            (suffix, suffix_in), (gsum_ref, gsum_in), (tsum_ref, tsum_in), (hsum_ref, hsum_in)
        ):
            out[...] = given[...]
        go[...] = join_states(go_refs, head_choice_t(inner, head_size), groups)
        gp[STRETCH : STRETCH + 8, :] = gp_in[...]
        pp[STRETCH : STRETCH + 8, :] = pp_in[...]

    @pl.when(step > 0)
    def _():
        gp[STRETCH : STRETCH + 8, :] = gp[0:8, :]
        pp[STRETCH : STRETCH + 8, :] = pp[0:8, :]

    @pl.when(c == 0)
    def _():
        mx[0:8, :] = edge_ref[HALO - 8 :, :].astype(f32)

    @pl.when(c > 0)
    def _():
        mx[0:8, :] = before_ref[HALO - 8 :, :].astype(f32)

    pos = column(pos_ref[0].astype(f32))
    pp[0:STRETCH, :] = pos
    mx[8 : 8 + STRETCH, :] = mixed_ref[...].astype(f32)
    values = vkq_ref[:, :inner]
    keys = vkq_ref[:, inner : inner + states]
    queries = vkq_ref[:, inner + states :]
    value_f = values.astype(f32)
    gssm = gssm_ref[...]
    g = gssm.astype(f32)
    step_pre = step_ref[...]
    decay = decay_ref[...]
    decay_t = decay.T
    dt = steps_of(step_pre, pos, heads)
    rate = -jnp.exp(rate_ref[...])
    choice = head_choice(inner, head_size)
    choice_t = head_choice_t(inner, head_size)
    dt_wide = dot_pair(dt, choice)
    dt_values = (value_f * dt_wide).astype(bf16)
    mask = mask_matrix(pos)
    gram = nt(queries, keys)
    per = LANES // head_size
    grad_gram = None
    turned = []
    for pair in range(inner // LANES):
        lanes = slice(pair * LANES, (pair + 1) * LANES)
        total = None
        for k in range(per):
            h = pair * per + k
            spread = jnp.exp((decay[:, h : h + 1] - decay_t[h : h + 1, :]) + mask)
            own_g = pair_sel(gssm[:, lanes], k, head_size)
            term = tn((gram * spread).astype(bf16), own_g)
            total = term if total is None else total + term
            more = nt(own_g, dt_values[:, lanes]) * spread
            grad_gram = more if grad_gram is None else grad_gram + more
        turned.append(total)
    turned = jnp.concatenate(turned, axis=1)
    grad_gram = grad_gram.astype(bf16)
    entering = state_ref[0]
    after = suffix[0:1, :]
    leaving = leave_ref[0] + head_column(after, choice_t) * go[...]
    leaving_low = leaving.astype(bf16)
    passing = passing_row(pos, decay)
    suffix[...] = suffix[...] * passing
    far = end_factor(pos, decay)
    wend = far * dt
    wend_wide = dot_pair(wend, choice)
    keyed = nt(keys, leaving_low)
    core = (g * dot_pair(carry_factor(pos, decay), choice)).astype(bf16)
    grad_values = skip_ref[...] * g + dt_wide * turned + wend_wide * keyed
    grad_keys = tn(grad_gram, queries) + nn((value_f * wend_wide).astype(bf16), leaving_low)
    grad_queries = nn(grad_gram, keys) + nn(core, entering)
    within_dt = dot_pair(value_f * turned, choice_t)
    within_logs = dot_pair(dt_values.astype(f32) * turned, choice_t)
    grad_wend = dot_pair(value_f * keyed, choice_t)
    through = jnp.sum(leaving * entering.astype(f32), axis=1, keepdims=True)
    last_grad = passing * jnp.sum(through * choice_t.astype(f32), axis=0, keepdims=True)
    end_terms = grad_wend * wend
    grad_logs = glog_ref[...] - within_logs - end_terms
    at_last = iota((STRETCH, LANES), 0) == STRETCH - 1
    grad_logs = grad_logs + jnp.where(
        at_last, jnp.sum(end_terms, axis=0, keepdims=True) + last_grad, 0.0
    )
    tri = (iota((STRETCH, STRETCH), 1) >= iota((STRETCH, STRETCH), 0)).astype(bf16)
    grad_steps = dot_triple(tri, grad_logs)
    grad_dt = within_dt + grad_wend * far + grad_steps * rate
    lane_ok = (iota((STRETCH, LANES), 1) < heads) & (pos >= 0.0)
    grad_step = jnp.where(lane_ok, grad_dt * jax.nn.sigmoid(step_pre), 0.0)
    hsum_ref[0:1, :] += jnp.sum(grad_step, axis=0, keepdims=True)
    hsum_ref[1:2, :] += jnp.sum(grad_steps * dt, axis=0, keepdims=True) * rate

    conv = conv_of(mx, taps_ref, pos)
    sig = jax.nn.sigmoid(conv)
    grad_conv = jnp.concatenate([grad_values, grad_keys, grad_queries], axis=1)
    grad_pre = grad_conv * (sig * (1.0 + conv * (1.0 - sig)))
    gp[0:STRETCH, :] = grad_pre
    tsum_ref[CONV : CONV + 1, :] += jnp.sum(grad_pre, axis=0, keepdims=True)
    tsum_ref[CONV - 1 : CONV, :] += jnp.sum(
        grad_pre * mx[8 : 8 + STRETCH, :], axis=0, keepdims=True
    )
    grad_mixed = grad_pre * taps_ref[CONV - 1 : CONV, :]
    for s in range(1, CONV):
        inside = (pos[:, :1] >= float(s)).astype(f32)
        tsum_ref[CONV - 1 - s : CONV - s, :] += jnp.sum(
            grad_pre * inside * mx[8 - s : 8 - s + STRETCH, :], axis=0, keepdims=True
        )
        later = (pp[s : s + STRETCH, :][:, :1] >= float(s)).astype(f32)
        grad_mixed = grad_mixed + gp[s : s + STRETCH, :] * later * taps_ref[
            CONV - 1 - s : CONV - s, :
        ]
    grads = jnp.concatenate(
        [ggate_ref[...], grad_mixed.astype(bf16), grad_step.astype(bf16)], axis=1
    )
    partial = nt(grads, w_ref[...])
    unit = row_norm(tok_ref[...].astype(f32))[1]
    grads_ref[...] = grads[:, at_mixed:]
    gp_out[...] = gp[0:8, :]
    pp_out[...] = pp[0:8, :]
    part_ref[...] = partial.astype(bf16)
    gsum_ref[0:1, :] += jnp.sum(partial * unit, axis=0, keepdims=True)
    ret_ref[...] = jnp.zeros_like(ret_ref)

    @pl.when(c == 0)
    def _():
        edge[0:8, :] = jnp.zeros((8, width), f32)
        total = jnp.zeros((8, width), f32)
        for s in range(1, CONV):
            inside = (pos[0:8, :1] >= float(s)).astype(f32)
            edge[8:16, :] = gp[0:8, :] * inside
            total = total + edge[s : s + 8, :] * taps_ref[CONV - 1 - s : CONV - s, :]
        ret_ref[...] = total


def spread_rows(out_ref, total_ref, groups, cores):
    size = total_ref.shape[0] // (cores * groups)
    for at in range(cores * groups):
        out_ref[at % cores, at // cores] = total_ref[at * size : (at + 1) * size, :].astype(bf16)


def first_grad_kernel(
    dims, groups, cores, tok_ref, gain_ref, gate_ref, og_ref, low_ref, out_ref, total
):
    inner = dims[2]
    c = pl.program_id(0)

    @pl.when(c == 0)
    def _():
        total[...] = jnp.zeros_like(total)

    normed = (row_norm(tok_ref[...].astype(f32))[1] * gain_ref[0:1, :]).astype(bf16)
    total[:, :inner] += tn(normed, gate_ref[...])
    total[:, inner:] += tn(og_ref[...], low_ref[...])

    @pl.when(c == pl.num_programs(0) - 1)
    def _():
        spread_rows(out_ref, total, groups, cores)


def weight_grad_kernel(
    dims, groups, cores,
    tok_ref, gain_ref, grads_ref, extra_ref, gsum_ref, tail_ref,
    out_ref,
    total,
):
    heads, head_size, inner, states = dims
    width = inner + 2 * states
    c = pl.program_id(0)

    @pl.when(c == 0)
    def _():
        total[...] = jnp.zeros_like(total)

    unit = row_norm(tok_ref[...].astype(f32))[1]
    normed = (unit * gain_ref[0:1, :]).astype(bf16)
    total[...] += tn(normed, grads_ref[...])

    @pl.when(c == pl.num_programs(0) - 1)
    def _():
        total[:, :width] += tn(normed[STRETCH - HALO :], extra_ref[...])
        norm = gsum_ref[0:1, :] + jnp.sum(
            tail_ref[...] * unit[STRETCH - HALO :], axis=0, keepdims=True
        )
        norm = jnp.broadcast_to(norm, (LANES, norm.shape[1])).T
        misc = total[:, width:]
        total[:, width:] = jnp.where(iota(misc.shape, 1) == heads, norm, misc)
        spread_rows(out_ref, total, groups, cores)


def pair_kernel(mine_ref, came_ref, after_ref, out_ref):
    out_ref[...] = (mine_ref[...].astype(f32) + came_ref[...].astype(f32)).astype(bf16)


def mixed_out_kernel(stats_ref, branch_ref, tok_ref, out_ref):
    scale = lax.rsqrt(column(stats_ref[...])[:, 0:1] / INNER + epsilon)
    out_ref[...] = (tok_ref[...].astype(f32) + scale * branch_ref[...].astype(f32)).astype(bf16)


def tokens_grad_kernel(grad_ref, tok_ref, og_ref, gain_ref, out_ref):
    scaling, unit = row_norm(tok_ref[...].astype(f32))
    grad = grad_ref[...].astype(f32) * gain_ref[0:1, :]
    mean = jnp.mean(grad * unit, axis=-1, keepdims=True)
    out_ref[...] = scaling * (grad - unit * mean) + og_ref[...].astype(f32)


def own_rows_kernel(mine_ref, came_ref, tok_ref, gain_ref, tail_ref, out_ref):
    scaling, unit = row_norm(tok_ref[...].astype(f32))
    grad = mine_ref[...].astype(f32) + came_ref[...].astype(f32)
    size, model = grad.shape
    tail = jnp.concatenate([jnp.zeros((size - HALO, model), f32), tail_ref[...]], axis=0)
    grad = grad + jnp.where(pl.program_id(0) == pl.num_programs(0) - 1, tail, 0.0)
    grad = grad * gain_ref[0:1, :]
    mean = jnp.mean(grad * unit, axis=-1, keepdims=True)
    out_ref[...] = (scaling * (grad - unit * mean)).astype(bf16)


def copy_kernel(in_ref, out_ref):
    out_ref[...] = in_ref[...]


def add_kernel(a_ref, b_ref, out_ref):
    out_ref[...] = a_ref[...].astype(f32) + b_ref[...].astype(f32)


def own_branch_kernel(stats_ref, mine_ref, came_ref, tok_ref, out_ref):
    scale = lax.rsqrt(column(stats_ref[...])[:, 0:1] / INNER + epsilon)
    branch = mine_ref[...].astype(f32) + came_ref[...].astype(f32)
    out_ref[...] = (tok_ref[...].astype(f32) + scale * branch).astype(bf16)


def per_device(
    tokens,
    norm_gain,
    inner_weight,
    state_weight,
    step_weight,
    inner_taps,
    state_taps,
    step_bias,
    log_rate,
    skip_gain,
    gated_gain,
    out_weight,
    out_grad,
    positions,
):
    shares = row_shares()
    share = lax.axis_index("tp") // (lax.axis_size("tp") // shares)
    all_rows, model = tokens.shape
    rows = all_rows // shares
    own_heads = step_bias.shape[0]
    own_inner = gated_gain.shape[0]
    head_size = own_inner // own_heads
    heads, inner = own_heads * shares, own_inner * shares
    states = state_weight.shape[1] // 2
    blocks = rows // STRETCH
    width = inner + 2 * states
    at_mixed, at_misc = inner, inner + width
    columns = at_misc + LANES
    dims = (heads, head_size, inner, states)
    parts = lax.axis_size("ctx") * shares

    def own_share(x, size):
        return x if shares == 1 else lax.dynamic_slice_in_dim(x, share * size, size)

    def joined(groups, begin, size):
        return [g[:, begin : begin + size] for g in groups]

    def steps_at(lane):
        return jnp.pad(step_weight, ((0, 0), (lane, LANES - lane - own_heads)))

    own_rows_of = norm_gain.shape[0]
    gain_lanes = jnp.concatenate(
        [
            jnp.zeros((own_rows_of, heads), bf16),
            norm_gain[:, None],
            jnp.zeros((own_rows_of, LANES - heads - 1), bf16),
        ],
        axis=1,
    )
    edge_rows = lax.ppermute(tokens[all_rows - HALO :], "ctx", [(0, 1)])
    all_tokens, all_grad = tokens, out_grad
    tokens, out_grad = own_share(tokens, rows), own_share(out_grad, rows)
    positions = own_share(positions, rows)
    halo_tokens = edge_rows
    if shares > 1:
        halo_tokens = jnp.where(share == 0, edge_rows, all_tokens[rows - HALO : rows])

    head_params = jnp.stack([step_bias, log_rate, skip_gain])
    small_own = jnp.concatenate(
        [
            jnp.pad(jnp.concatenate([inner_taps, gated_gain[None]]), ((0, 8 - CONV - 2), (0, 0))),
            jnp.pad(head_params, ((0, 5), (0, LANES - own_heads))),
        ],
        axis=1,
    )
    channels_in = [inner_weight[0], inner_weight[1]]
    near = gather_near(
        jnp.concatenate(channels_in + [state_weight, steps_at(0) + gain_lanes], axis=1)
    )
    stacks = gather_stacks(near)
    count = len(stacks)
    out_near = out_weight.T
    if shares > 1:
        more = swap_tp(jnp.concatenate(channels_in + [steps_at(own_heads)], axis=1), 2)
        near = gather_near(tied(more, tokens, out_grad, halo_tokens))
        out_more = swap_tp(tied(out_near, more), 2)
        small_more = swap_tp(tied(small_own, more), 2)
        near[-1] = tied(near[-1], out_more, small_more)
        stacks += gather_stacks(near)
        out_near = jnp.concatenate([out_near, out_more], axis=1)
    out_near = gather_near(tied(out_near, near[-1]))
    place = gather_place(own_rows_of)

    small_groups = [small_own] + ([small_more] if shares > 1 else [])
    channel_rows = jnp.concatenate(joined(small_groups, 0, own_inner), axis=1)
    head_rows = jnp.concatenate(joined(small_groups, own_inner, own_heads), axis=1)
    taps = jnp.concatenate(
        [channel_rows, jnp.pad(state_taps, ((0, 8 - CONV - 1), (0, 0)))], axis=1
    )
    gain_row = channel_rows[CONV + 1 : CONV + 2]
    skip_row = jnp.repeat(head_rows[2], head_size)[None, :]
    head_rows = jnp.pad(head_rows, ((0, 0), (0, LANES - heads)))
    bias_row, rate_row = head_rows[0:1], head_rows[1:2]
    pos_rows = positions.reshape(blocks, 1, STRETCH)

    def fixed(shape):
        return pl.BlockSpec(shape, lambda c: (0,) * len(shape))

    def by_rows(cols, order, at=0):
        return pl.BlockSpec((STRETCH, cols), lambda c: (order(c), at))

    def by_block(order):
        return pl.BlockSpec((1, inner, states), lambda c: (order(c), 0, 0))

    def pos_spec(order):
        return pl.BlockSpec((1, 1, STRETCH), lambda c: (order(c), 0, 0))

    def ahead(c):
        return c

    def reverse(c):
        return blocks - 1 - c

    def shape(*dims_of, dtype=f32):
        return jax.ShapeDtypeStruct(dims_of, dtype)

    light = pl.CostEstimate(flops=1024, bytes_accessed=1024, transcendentals=0)
    params = pltpu.CompilerParams(
        dimension_semantics=("arbitrary",), vmem_limit_bytes=VMEM_BYTES
    )

    scalars = pl.BlockSpec(memory_space=pltpu.SMEM)
    mixed, vkq, ssm_local, step_pre, decay, enter, last_state, edge, model_gain, weight = (
        pl.pallas_call(
            functools.partial(forward_kernel, dims, count, shares),
            grid=(blocks,),
            in_specs=[
                scalars,
                *[fixed(a.shape) for a in stacks],
                pos_spec(ahead),
                by_rows(model, ahead),
                fixed((HALO, model)),
                fixed((8, width)),
                fixed((1, LANES)),
                fixed((1, LANES)),
                fixed((1, inner)),
            ],
            out_specs=[
                by_rows(width, ahead),
                by_rows(width, ahead),
                by_rows(inner, ahead),
                by_rows(LANES, ahead),
                by_rows(LANES, ahead),
                by_block(ahead),
                fixed((inner + HALO, states)),
                fixed((HALO, width)),
                fixed((8, model)),
                fixed((model, columns)),
            ],
            out_shape=[
                shape(rows, width, dtype=bf16),
                shape(rows, width, dtype=bf16),
                shape(rows, inner),
                shape(rows, LANES),
                shape(rows, LANES),
                shape(blocks, inner, states),
                shape(inner + HALO, states, dtype=bf16),
                shape(HALO, width, dtype=bf16),
                shape(8, model),
                shape(model, columns, dtype=bf16),
            ],
            scratch_shapes=[
                pltpu.VMEM((STRETCH + 8, width), f32),
                pltpu.VMEM((inner, states), f32),
                pltpu.VMEM((8, LANES), f32),
            ],
            compiler_params=params,
            name="forward",
        )(
            place, *stacks, pos_rows, tokens, halo_tokens, taps, bias_row, rate_row, skip_row
        )
    )
    out_stacks = gather_stacks(out_near[:-1] + [tied(out_near[-1], last_state)])
    coming = [shift_part(last_state, by) for by in range(1, parts)]
    gate, grad_out, out_t = pl.pallas_call(
        functools.partial(gates_kernel, count),
        grid=(blocks,),
        in_specs=[
            scalars,
            *[fixed(a.shape) for a in out_stacks],
            by_rows(model, ahead),
            fixed((8, model)),
            pl.BlockSpec((model, inner), lambda c: (0, 0)),
            by_rows(model, ahead),
        ],
        out_specs=[by_rows(inner, ahead), by_rows(inner, ahead), fixed((model, inner))],
        out_shape=[shape(rows, inner), shape(rows, inner), shape(model, inner, dtype=bf16)],
        compiler_params=params,
        name="gates",
    )(place, *out_stacks, tokens, model_gain, weight, out_grad)
    ssm, state, stats, branch = pl.pallas_call(
        functools.partial(stats_kernel, dims, shares, parts - 1),
        grid=(blocks,),
        in_specs=[
            *[fixed((inner + HALO, states))] * (parts - 1),
            pos_spec(ahead),
            by_rows(inner, ahead),
            by_rows(inner, ahead),
            by_rows(states, ahead, (inner + states) // states),
            by_rows(LANES, ahead),
            by_block(ahead),
            by_rows(inner, ahead),
            fixed((model, inner)),
            fixed((1, inner)),
        ],
        out_specs=[
            by_rows(inner, ahead),
            by_block(ahead),
            pl.BlockSpec((2, STRETCH), lambda c: (0, c)),
            by_rows(model, ahead),
        ],
        out_shape=[
            shape(rows, inner),
            shape(blocks, inner, states, dtype=bf16),
            shape(2, rows),
            shape(rows, model, dtype=bf16),
        ],
        scratch_shapes=[pltpu.VMEM((8, LANES), f32), pltpu.VMEM((inner, states), f32)],
        compiler_params=params,
        name="stats",
    )(*coming, pos_rows, ssm_local, gate, vkq, decay, enter, grad_out, out_t, gain_row)
    half = rows // 2
    member = lax.axis_index("tp") % 2

    def halves(x):
        sent = lax.dynamic_slice_in_dim(x, (1 - member) * half, half)
        return lax.dynamic_slice_in_dim(tied(x, sent), member * half, half), swap_tp(sent, 1)

    if shares > 1:
        own_tokens = lax.dynamic_slice_in_dim(tokens, member * half, half)
        stats = stats + swap_tp(stats, 1)
        own_branch = pl.pallas_call(
            own_branch_kernel,
            grid=(half // STRETCH,),
            in_specs=[pl.BlockSpec((2, STRETCH), lambda c: (0, c))]
            + [by_rows(model, ahead)] * 3,
            out_specs=by_rows(model, ahead),
            out_shape=shape(half, model, dtype=bf16),
            compiler_params=params,
            name="own_branch",
        )(
            lax.dynamic_slice_in_dim(stats, member * half, half, 1),
            *halves(tied(branch, stats)),
            own_tokens,
        )
    else:
        stats = sum_tp_small(stats)
        first_total = lax.psum(branch, "tp")
    grad_ssm, grad_gate, normed_out, grad_logs, leave, last_back, gate_sums = pl.pallas_call(
        functools.partial(gate_back_kernel, dims, shares),
        grid=(blocks,),
        in_specs=[
            pos_spec(reverse),
            pl.BlockSpec((2, STRETCH), lambda c: (0, reverse(c))),
            by_rows(inner, reverse),
            by_rows(inner, reverse),
            by_rows(inner, reverse),
            by_rows(width, reverse),
            by_rows(LANES, reverse),
            fixed((1, inner)),
            fixed((1, inner)),
        ],
        out_specs=[
            by_rows(inner, reverse),
            by_rows(inner, reverse),
            by_rows(inner, reverse),
            by_rows(LANES, reverse),
            by_block(reverse),
            fixed((inner + HALO, states)),
            fixed((8, inner)),
        ],
        out_shape=[
            shape(rows, inner, dtype=bf16),
            shape(rows, inner, dtype=bf16),
            shape(rows, inner, dtype=bf16),
            shape(rows, LANES),
            shape(blocks, inner, states),
            shape(inner + HALO, states, dtype=bf16),
            shape(8, inner),
        ],
        scratch_shapes=[pltpu.VMEM((inner, states), f32), pltpu.VMEM((8, LANES), f32)],
        compiler_params=params,
        cost_estimate=light,
        name="gate_back",
    )(pos_rows, stats, ssm, gate, grad_out, vkq, decay, gain_row, skip_row)
    going = [shift_part(last_back, -by) for by in range(1, parts)]
    if shares > 1:
        first_gather = lax.all_gather(tied(own_branch, *going), "tp", axis=0, tiled=True)
        mixed_out = pl.pallas_call(
            copy_kernel,
            grid=(all_rows // STRETCH,),
            in_specs=[by_rows(model, ahead)],
            out_specs=by_rows(model, ahead),
            out_shape=shape(all_rows, model, dtype=bf16),
            compiler_params=params,
            name="mixed_out",
        )(first_gather)
        first_total = first_gather[:8, :LANES]
    near_count, cores = (lax.axis_size("fsdp"), lax.axis_size("ctx")) if small_mesh() else (1, 1)

    def grad_shape(cols):
        return (cores, near_count, model // (cores * near_count), cols)

    per_halo = STRETCH // HALO

    def scan_piece(first, size, going, carried):
        def place_of(c):
            return blocks - 1 - first - c

        grads_before, *carried = carried
        carry_shapes = [a.shape for a in carried]
        aliases = {}
        in_specs = [
            pos_spec(place_of),
            by_rows(model, place_of),
            fixed((model, columns)),
            fixed((8, model)),
            fixed((8, width)),
            fixed((1, LANES)),
            fixed((1, inner)),
            by_rows(width, place_of),
            pl.BlockSpec(
                (HALO, width), lambda c: (jnp.maximum(place_of(c) * per_halo - 1, 0), 0)
            ),
            fixed((HALO, width)),
            by_rows(width, place_of),
            by_rows(inner, place_of),
            by_rows(inner, place_of),
            by_rows(LANES, place_of),
            by_rows(LANES, place_of),
            by_rows(LANES, place_of),
            by_block(place_of),
            by_block(place_of),
            *[fixed(a) for a in carry_shapes],
            *[fixed((inner + HALO, states))] * (parts - 1),
        ]
        operands = [
            pos_rows, tokens, weight, model_gain, taps, rate_row, skip_row, mixed, mixed, edge,
            vkq, grad_ssm, grad_gate, grad_logs, step_pre, decay, state, leave, *carried, *going,
        ]
        if grads_before is not None:
            aliases = {len(operands): 2}
            operands.append(grads_before)
            in_specs.append(pl.BlockSpec(memory_space=pl.ANY))
        return pl.pallas_call(
            functools.partial(scan_back_kernel, dims, first, blocks, shares, parts - 1),
            grid=(size,),
            in_specs=in_specs,
            out_specs=[
                pl.BlockSpec((STRETCH, model), lambda c: (size - 1 - c, 0)),
                fixed((8, width)),
                by_rows(columns - inner, place_of),
                *[fixed(a) for a in carry_shapes],
            ],
            out_shape=[
                shape(size * STRETCH, model, dtype=bf16),
                shape(8, width),
                shape(rows, columns - inner, dtype=bf16),
                *[shape(*a) for a in carry_shapes],
            ],
            input_output_aliases=aliases,
            scratch_shapes=[
                pltpu.VMEM((STRETCH + 8, width), f32),
                pltpu.VMEM((STRETCH + 8, width), f32),
                pltpu.VMEM((STRETCH + 8, LANES), f32),
                pltpu.VMEM((16, width), f32),
                pltpu.VMEM((inner, states), f32),
            ],
            compiler_params=params,
            cost_estimate=light,
        name="scan_back",
        )(*operands)

    carried = [
        None,
        jnp.zeros((8, width), f32),
        jnp.zeros((8, LANES), f32),
        jnp.ones((8, LANES), f32),
        jnp.zeros((8, model), f32),
        jnp.zeros((8, width), f32),
        jnp.zeros((8, LANES), f32),
    ]
    partial, returned, *carried = scan_piece(0, blocks, going, carried)
    grads, _, _, _, norm_sums, tap_sums, head_sums = carried

    small = jnp.concatenate([tap_sums.reshape(-1, LANES), gate_sums.reshape(-1, LANES), head_sums])
    if shares > 1:
        mine, came = halves(partial)
        small = tied(small, mine)
        normed_out = tied(normed_out, mine)
    first_grad = pl.pallas_call(
        functools.partial(first_grad_kernel, dims, near_count, cores),
        grid=(blocks,),
        in_specs=[
            by_rows(model, ahead),
            fixed((8, model)),
            by_rows(inner, ahead),
            by_rows(model, ahead),
            by_rows(inner, ahead),
        ],
        out_specs=fixed(grad_shape(2 * inner)),
        out_shape=shape(*grad_shape(2 * inner), dtype=bf16),
        scratch_shapes=[pltpu.VMEM((model, 2 * inner), f32)],
        compiler_params=params,
        cost_estimate=light,
        name="first_grad",
    )(tokens, model_gain, grad_gate, out_grad, normed_out)
    small = sum_rows_group(small)
    extra = shift_part(returned, -1).astype(bf16)
    if shares > 1:
        extra = jnp.concatenate(
            [extra[:, own_inner:inner], extra[:, :own_inner], extra[:, inner:]], axis=1
        )
    extra = jnp.concatenate([jnp.zeros((HALO - 8, width), bf16), extra], axis=0)
    tail_part = nt(extra, weight[:, at_mixed:at_misc])

    if shares > 1:
        tail_low = tail_part.astype(bf16)
        tail_sum = tail_low.astype(f32) + swap_tp(tail_low, 1).astype(f32)
        tail_sum = jnp.where(member == 1, tail_sum, 0.0)
        own_rows = pl.pallas_call(
            own_rows_kernel,
            grid=(half // STRETCH,),
            in_specs=[by_rows(model, ahead)] * 3 + [fixed((8, model)), fixed((HALO, model))],
            out_specs=by_rows(model, ahead),
            out_shape=shape(half, model, dtype=bf16),
            compiler_params=params,
            name="own_rows",
        )(tied(mine, first_grad), came, own_tokens, model_gain, tail_sum)
        grads = tied(grads, own_rows, first_total)
        own_rows = tied(own_rows, first_total)
        second_total = lax.all_gather(own_rows, "tp", axis=0, tiled=True)
    else:
        partial = partial.at[rows - HALO :].add(tail_part.astype(bf16))
        partial = tied(partial, first_total)
        mixed_out = pl.pallas_call(
            mixed_out_kernel,
            grid=(blocks,),
            in_specs=[
                pl.BlockSpec((2, STRETCH), lambda c: (0, c)),
                by_rows(model, ahead),
                by_rows(model, ahead),
            ],
            out_specs=by_rows(model, ahead),
            out_shape=shape(rows, model, dtype=bf16),
            compiler_params=params,
            name="mixed_out",
        )(stats, first_total, tokens)
        tokens_grad = pl.pallas_call(
            tokens_grad_kernel,
            grid=(blocks,),
            in_specs=[by_rows(model, ahead)] * 3 + [fixed((8, model))],
            out_specs=by_rows(model, ahead),
            out_shape=shape(rows, model),
            compiler_params=params,
            name="tokens_grad",
        )(lax.psum(partial, "tp"), tokens, out_grad, model_gain)

    weight_grad = pl.pallas_call(
        functools.partial(weight_grad_kernel, dims, near_count, cores),
        grid=(blocks,),
        in_specs=[
            by_rows(model, ahead),
            fixed((8, model)),
            by_rows(columns - inner, ahead),
            fixed((HALO, width)),
            fixed((8, model)),
            fixed((HALO, model)),
        ],
        out_specs=fixed(grad_shape(columns - inner)),
        out_shape=shape(*grad_shape(columns - inner), dtype=bf16),
        scratch_shapes=[pltpu.VMEM((model, columns - inner), f32)],
        compiler_params=params,
        cost_estimate=light,
        name="weight_grad",
    )(tokens, model_gain, grads, extra, norm_sums, tail_part)
    first_grad = scatter_rows(first_grad)
    if shares > 1:
        tokens_grad = pl.pallas_call(
            add_kernel,
            grid=(all_rows // STRETCH,),
            in_specs=[by_rows(model, ahead)] * 2,
            out_specs=by_rows(model, ahead),
            out_shape=shape(all_rows, model),
            compiler_params=params,
            name="tokens_grad",
        )(second_total, all_grad)
    late_grad = scatter_rows(weight_grad)
    at = 8 * width // LANES
    tap_total = small[:at].reshape(8, width)
    gate_total = small[at : at + 8 * inner // LANES].reshape(8, inner)
    head_total = small[at + 8 * inner // LANES :]
    shared = late_grad[:, inner:].astype(bf16)
    state_taps_grad = tap_total[: CONV + 1, inner:]
    rows_of = jnp.concatenate([tap_total[: CONV + 1, :inner], gate_total[:2]])
    channels_of = [first_grad[:, :inner], late_grad[:, :inner], first_grad[:, inner:]]
    steps_of_grad = late_grad[:, width:]
    groups = [g[:, :own_inner] for g in channels_of] + [steps_of_grad[:, :own_heads]]
    channel_total, head_total = rows_of[:, :own_inner], head_total[:2, :LANES]
    if shares > 1:
        sent = [g[:, own_inner:] for g in channels_of]
        sent.append(steps_of_grad[:, own_heads:])
        sent.append(jnp.zeros((steps_of_grad.shape[0], own_heads), f32))
        sent = jnp.concatenate(sent, axis=1).astype(bf16)
        few = jnp.concatenate(
            [
                jnp.pad(rows_of[:, own_inner:], ((0, 1), (0, 0))),
                jnp.pad(
                    head_total[:, own_heads : own_heads + LANES // 2], ((0, 6), (0, LANES // 2))
                ),
            ],
            axis=1,
        )
        pair = pl.pallas_call(
            pair_kernel,
            grid=(1,),
            in_specs=[fixed(shared.shape)] * 2 + [pl.BlockSpec(memory_space=pl.ANY)],
            out_specs=fixed(shared.shape),
            out_shape=shape(*shared.shape, dtype=bf16),
            compiler_params=params,
            name="pair",
        )(shared, swap_tp(shared, 1), tokens_grad)
        taps_pair = state_taps_grad + swap_tp(state_taps_grad, 1)
        came, few = swap_tp(sent, 2).astype(f32), swap_tp(few, 2)
        groups = [
            g + came[:, k * own_inner : k * own_inner + g.shape[1]] for k, g in enumerate(groups)
        ]
        channel_total = channel_total + few[: CONV + 3, :own_inner]
        head_total = head_total[:, :own_heads] + few[:2, own_inner : own_inner + own_heads]
        shared = pair.astype(f32) + swap_tp(pair, 2).astype(f32)
        state_taps_grad = taps_pair + swap_tp(taps_pair, 2)
    else:
        shared = sum_tp_small(shared)
        state_taps_grad = sum_tp_small(state_taps_grad)
        head_total = head_total[:, :own_heads]
    state_weight_grad = shared[:, : 2 * states]
    norm_gain_grad = shared[:, 2 * states + heads]
    inner_weight_grad = jnp.stack(groups[:2])
    out_weight_grad = groups[2].T
    return (
        mixed_out,
        tokens_grad,
        norm_gain_grad,
        inner_weight_grad,
        state_weight_grad,
        groups[3],
        channel_total[: CONV + 1],
        state_taps_grad,
        head_total[0],
        head_total[1],
        jnp.sum(channel_total[CONV + 2].reshape(own_heads, head_size), axis=1),
        channel_total[CONV + 1],
        out_weight_grad,
    )


def solution(mesh):
    return jax.shard_map(
        per_device,
        mesh=mesh,
        in_specs=(
            P(("fsdp", "ctx"), None),
            P(("fsdp", "ctx")),
            P(None, ("fsdp", "ctx"), "tp"),
            P(("fsdp", "ctx"), None),
            P(("fsdp", "ctx"), "tp"),
            P(None, "tp"),
            P(),
            P("tp"),
            P("tp"),
            P("tp"),
            P("tp"),
            P("tp", ("fsdp", "ctx")),
            P(("fsdp", "ctx"), None),
            P(("fsdp", "ctx")),
        ),
        out_specs=(
            P(("fsdp", "ctx"), None),
            P(("fsdp", "ctx"), None),
            P(("fsdp", "ctx")),
            P(None, ("fsdp", "ctx"), "tp"),
            P(("fsdp", "ctx"), None),
            P(("fsdp", "ctx"), "tp"),
            P(None, "tp"),
            P(),
            P("tp"),
            P("tp"),
            P("tp"),
            P("tp"),
            P("tp", ("fsdp", "ctx")),
        ),
        check_vma=False,
    )
```
